256 devices in a mesh: dp: 64 (over y, z, core), tensor: 4 (over x).
Axes of the slice: x: 4, y: 4, z: 8, core: 2. Of those that a mesh axis runs over, the one named last changes fastest.
Arguments:
- hidden: bfloat16 [16384, 14336], P('dp', 'tensor')
- upstream: bfloat16 [16384, 8192], P('dp'), may hold values from -6 to 6
- adapter_down_weight: bfloat16 [14336, 128], P('tensor'), may hold values from -0.046875 to 0.046875
- adapter_up_weight: bfloat16 [128, 8192], replicated, may hold values from -0.0625 to 0.0625
- token_user_slot: int32 [16384], P('dp'), may hold values from 0 to 7
- padding_token_mask: int32 [16384], P('dp'), may hold values 0 or 1
- overflow_user_rows: int32 [64, 64], P('dp'), may hold values from 0 to 255, as said below
- overflow_home_index: int32 [64, 64], P('dp'), may hold values from 0 to 63, as said below
Outputs:
- lora_a_grad: float32 [4, 3584, 128], P('tensor', 'dp')
- lora_b_grad: float32 [4, 2048, 128], P('tensor', 'dp')
The draws below stay inside these ranges and needn't reach their ends.
Inputs may be any that keep to these rules, and one draw needn't show every extreme that they name: `overflow_user_rows`: the listed rows of one data index are distinct. `overflow_home_index`: among one data index's listed rows no home is named more than 2 times; in every draw one home is named 2 times by every data index.
All inputs are finite; a program needn't handle non-finite values. No bound on the sum of `padding_token_mask` on one device may be relied on, other than what follows from the above.
Results may differ from the reference program's by a relative error of at most 0.0029.
The reference program's roundings to bfloat16 on the way count: a program that leaves them out, or rounds other values in their place, can miss the bound.
Values may be sent and summed in bfloat16 or wider, within the bound.
No kernel may reach another device: no remote copies, remote signals or barrier semaphores. Data moves between devices by JAX's collectives and lax.ppermute only.
A program may use at most 64 MiB of HBM per device.

```python
import math
import jax
import jax.numpy as jnp
from jax import lax

MODEL_WIDTH = 8192
HIDDEN_UNITS = 14336
ADAPTER_RANK = 128
TOK_DEV = 256
U_DEV = 8
SLOT = 2
TOKENS = 16384
N_DP = 64
N_TENSOR = 4


def spill_plan(key):
    spill_count = N_DP * SLOT // 2
    row_keys = jax.random.split(jax.random.fold_in(key, 101), N_DP)
    row_list = jax.vmap(lambda one_key: jax.random.permutation(one_key, TOK_DEV)[:spill_count])(row_keys).astype(jnp.int32)
    busy_home = jax.random.randint(jax.random.fold_in(key, 102), (), 0, N_DP).astype(jnp.int32)
    home_keys = jax.random.split(jax.random.fold_in(key, 103), N_DP)
    shuffles = jax.vmap(lambda one_key: jax.random.permutation(one_key, N_DP))(home_keys).astype(jnp.int32)
    priority = jnp.where(shuffles == busy_home, -1, jnp.arange(N_DP, dtype=jnp.int32)[None, :])
    ordered = jnp.take_along_axis(shuffles, jnp.argsort(priority, axis=1), axis=1)
    picked = ordered[:, :spill_count // SLOT]
    home_list = jnp.repeat(picked, SLOT, axis=1)
    mix_keys = jax.random.split(jax.random.fold_in(key, 104), N_DP)
    home_list = jax.vmap(lambda one_key, homes_row: homes_row[jax.random.permutation(one_key, spill_count)])(mix_keys, home_list)
    return (row_list, home_list.astype(jnp.int32))


def draw_overflow_user_rows(key, part):
    row_list, home_list = spill_plan(key)
    return row_list


def draw_overflow_home_index(key, part):
    row_list, home_list = spill_plan(key)
    return home_list


def draw_token_user_slot(key, part):
    row_list, home_list = spill_plan(key)
    key = jax.random.fold_in(key, 7)
    first_key, second_key = jax.random.split(key)
    own_users = jax.random.randint(first_key, (N_DP, TOK_DEV), 0, U_DEV).astype(jnp.int32)
    heavy_users = jax.random.randint(second_key, home_list.shape, 0, 2).astype(jnp.int32)
    user_ids = jax.vmap(lambda users_row, rows_row, heavy_row: users_row.at[rows_row].set(heavy_row))(own_users, row_list, heavy_users)
    return user_ids.reshape(-1)


def draw_hidden(key, part):
    key = jax.random.fold_in(key, 11)
    value_key, scale_key = jax.random.split(key, 2)
    scales = jnp.exp(jax.random.uniform(scale_key, (TOKENS, 1), jnp.float32, math.log(0.3), math.log(3.0)))
    values = jax.random.normal(value_key, (TOKENS, HIDDEN_UNITS), jnp.float32) * scales
    return values.astype(jnp.bfloat16)


def touch_ends(entries, key, least, top_value):
    index_at = [jax.random.randint(jax.random.fold_in(key, axis), (), 0, length) for axis, length in enumerate(entries.shape)]
    widest = entries.shape.index(max(entries.shape))
    next_to = index_at[:widest] + [(index_at[widest] + 1) % entries.shape[widest]] + index_at[widest + 1:]
    return entries.at[tuple(index_at)].set(least).at[tuple(next_to)].set(top_value)


def shard_levels(key, extent, pieces, low, top_value):
    def one(position, blocks):
        steps = jax.random.uniform(jax.random.fold_in(jax.random.fold_in(key, 6), position), (blocks,), jnp.float32, low / len(pieces), top_value / len(pieces))
        return jnp.repeat(jnp.exp(steps), extent[position] // blocks).reshape((-1,) + (1,) * (len(extent) - position - 1))

    level = one(*pieces[0])
    for cut in pieces[1:]:
        level = level * one(*cut)
    return level


def centred(own_key, dims, deviation, reach, cuts=(), kind=jnp.bfloat16):
    values = jax.random.normal(own_key, dims, jnp.float32) * deviation
    if len(cuts) > 0:
        values = shard_levels(own_key, dims, cuts, -0.22, 0.18) * values
    return jnp.clip(values, min=-reach, max=reach).astype(kind)


def setup_inputs(seed: int = 0) -> dict:
    arg_keys = jax.random.split(jax.random.key(seed), 9)
    return {
        "hidden": draw_hidden(jax.random.fold_in(arg_keys[8], 71), 0),
        "upstream": centred(arg_keys[1], (TOKENS, MODEL_WIDTH), 1.0, 6.0, ((0, 64),)),
        "adapter_down_weight": centred(arg_keys[2], (HIDDEN_UNITS, ADAPTER_RANK), HIDDEN_UNITS ** -0.5, 0.046875, ((0, 4),)),
        "adapter_up_weight": centred(arg_keys[3], (ADAPTER_RANK, MODEL_WIDTH), MODEL_WIDTH ** -0.5, 0.0625),
        "token_user_slot": draw_token_user_slot(jax.random.fold_in(arg_keys[8], 71), 0),
        "padding_token_mask": touch_ends((jax.random.randint(arg_keys[5], (TOKENS,), 0, 8) < 7).astype(jnp.int32), jax.random.fold_in(arg_keys[5], 1), 0, 1),
        "overflow_user_rows": draw_overflow_user_rows(jax.random.fold_in(arg_keys[8], 71), 0),
        "overflow_home_index": draw_overflow_home_index(jax.random.fold_in(arg_keys[8], 71), 0),
    }


CLIP_FACTOR = 4.0

def row_gram(rows):
    return lax.dot_general(rows, rows, (((1,), (1,)), ((), ())), preferred_element_type=jnp.float32)

def reference(hidden, upstream, adapter_down_weight, adapter_up_weight, token_user_slot, padding_token_mask, overflow_user_rows, overflow_home_index):
    users_all = U_DEV * N_DP
    clip_norm = CLIP_FACTOR * math.sqrt(ADAPTER_RANK * (HIDDEN_UNITS + MODEL_WIDTH))
    lowrank_product = jnp.dot(hidden, adapter_down_weight, preferred_element_type=jnp.float32).astype(jnp.bfloat16)
    backward_rank_term = lax.dot_general(upstream, adapter_up_weight, (((1,), (1,)), ((), ())), preferred_element_type=jnp.float32).astype(jnp.bfloat16)
    spill_count = overflow_user_rows.shape[1]
    positions = jnp.arange(spill_count, dtype=jnp.int32)
    same_home = overflow_home_index[:, :, None] == overflow_home_index[:, None, :]
    before = positions[None, :] < positions[:, None]
    rank_in = lax.optimization_barrier(jnp.sum((same_home & before[None]).astype(jnp.int32), axis=2))
    sources = jnp.arange(N_DP, dtype=jnp.int32)[:, None]
    global_row = (sources * TOK_DEV + overflow_user_rows).astype(jnp.int32)
    flat_slot = (overflow_home_index * (N_DP * SLOT) + sources * SLOT + rank_in).astype(jnp.int32).reshape(-1)
    slot_table = jnp.full((N_DP * N_DP * SLOT,), -1, jnp.int32).at[flat_slot].set(global_row.reshape(-1))
    slot_table = slot_table.reshape(N_DP, N_DP * SLOT)
    listed = jnp.zeros((N_DP * TOK_DEV,), jnp.int32).at[global_row.reshape(-1)].set(1)
    row_home = jnp.repeat(jnp.arange(N_DP, dtype=jnp.int32), TOK_DEV)
    row_home = row_home.at[global_row.reshape(-1)].set(overflow_home_index.reshape(-1).astype(jnp.int32))
    user_global = row_home * U_DEV + token_user_slot

    def per_home(home):
        local_rows = (home * TOK_DEV + jnp.arange(TOK_DEV, dtype=jnp.int32)).astype(jnp.int32)
        far_rows = slot_table[home]
        valid_slot = (far_rows >= 0).astype(jnp.int32)
        far_index = jnp.maximum(far_rows, 0).astype(jnp.int32)
        row_index = jnp.concatenate([local_rows, far_index])
        live_flag = jnp.concatenate([padding_token_mask[local_rows] * (1 - listed[local_rows]), valid_slot * padding_token_mask[far_index]]).astype(jnp.float32)
        slot_ids = token_user_slot[row_index]
        same_user = (slot_ids[:, None] == slot_ids[None, :]).astype(jnp.float32) * live_flag[:, None] * live_flag[None, :]
        pair_terms = same_user * (row_gram(hidden[row_index]) * row_gram(backward_rank_term[row_index]) + row_gram(lowrank_product[row_index]) * row_gram(upstream[row_index]))
        member = (jnp.arange(U_DEV, dtype=jnp.int32)[:, None] == slot_ids[None, :]).astype(jnp.float32) * live_flag[None, :]
        return jnp.dot(member, lax.optimization_barrier(jnp.sum(pair_terms, axis=1)), precision=lax.Precision.HIGHEST)
    norm_sq = lax.map(per_home, jnp.arange(N_DP, dtype=jnp.int32)).reshape(-1)
    factor = clip_norm / jnp.maximum(jnp.sqrt(norm_sq), clip_norm)
    weight = padding_token_mask.astype(jnp.float32) * factor[user_global] / users_all
    scaled_back = (weight[:, None] * backward_rank_term.astype(jnp.float32)).astype(jnp.bfloat16)
    scaled_up = (weight[:, None] * upstream.astype(jnp.float32)).astype(jnp.bfloat16)
    grad_a = lax.dot_general(hidden, scaled_back, (((0,), (0,)), ((), ())), preferred_element_type=jnp.float32)
    grad_b = lax.dot_general(scaled_up, lowrank_product, (((0,), (0,)), ((), ())), preferred_element_type=jnp.float32)
    return (grad_a.reshape(N_TENSOR, HIDDEN_UNITS // N_TENSOR, ADAPTER_RANK), grad_b.reshape(N_TENSOR, MODEL_WIDTH // N_TENSOR, ADAPTER_RANK))
```

```python
import math

import jax
import jax.numpy as jnp
from jax import lax
from jax.sharding import Mesh, PartitionSpec as P

MODEL_WIDTH = 8192
HIDDEN_UNITS = 14336
ADAPTER_RANK = 128
U_DEV = 8
SLOT = 2
CLIP_FACTOR = 4.0
N_Y = 4
N_Z = 8
N_CORE = 2
N_TENSOR = 4
DP = ("y", "z", "core")
f32 = jnp.float32
bf16 = jnp.bfloat16


def row_gram(rows):
    return lax.dot_general(rows, rows, (((1,), (1,)), ((), ())), preferred_element_type=f32)


def column_term(left_rows, right_rows):
    return lax.dot_general(
        left_rows, right_rows, (((0,), (0,)), ((), ())), preferred_element_type=f32
    )


def tensor_sum(part):
    got = [
        lax.ppermute(part, "tensor", [(i, (i + k) % N_TENSOR) for i in range(N_TENSOR)])
        for k in (1, 3, 2)
    ]
    return part + got[0] + got[1] + got[2]


def per_device(
    hidden,
    upstream,
    adapter_down_weight,
    adapter_up_weight,
    token_user_slot,
    padding_token_mask,
    overflow_user_rows,
    overflow_home_index,
):
    tokens_here = hidden.shape[0]
    n_data = N_Y * N_Z * N_CORE
    quarter = MODEL_WIDTH // N_TENSOR
    units = HIDDEN_UNITS // N_TENSOR
    tensor_index = lax.axis_index("tensor")
    core_index = lax.axis_index("core")
    total_users = U_DEV * n_data
    slots_all = n_data * SLOT
    clip_norm = CLIP_FACTOR * math.sqrt(ADAPTER_RANK * (HIDDEN_UNITS + MODEL_WIDTH))

    listed_rows = overflow_user_rows[0]
    listed_home = overflow_home_index[0]
    positions = jnp.arange(listed_rows.shape[0], dtype=jnp.int32)
    same_home = listed_home[:, None] == listed_home[None, :]
    before = positions[None, :] < positions[:, None]
    rank_in = jnp.sum((same_home & before).astype(jnp.int32), axis=1)
    slot_of = listed_home * SLOT + rank_in
    row_hit = listed_rows[:, None] == jnp.arange(tokens_here, dtype=jnp.int32)[None, :]
    token_slot = jnp.sum(jnp.where(row_hit, slot_of[:, None] + 1, 0), axis=0) - 1
    real = padding_token_mask > 0
    dispatch = (
        (jnp.arange(slots_all, dtype=jnp.int32)[:, None] == token_slot[None, :]) & real[None, :]
    ).astype(bf16)
    local_live = (real & (token_slot < 0)).astype(f32)

    own_cols = lax.dynamic_slice_in_dim(upstream, tensor_index * quarter, quarter, 1)
    rows = jnp.concatenate([hidden, own_cols], axis=1)
    send_rows = jnp.dot(dispatch, rows, preferred_element_type=f32).astype(bf16)
    got_rows = lax.all_to_all(
        send_rows.reshape(n_data, SLOT, -1), DP, 0, 0, tiled=True
    ).reshape(slots_all, -1)

    low = tensor_sum(jnp.dot(hidden, adapter_down_weight, preferred_element_type=f32)).astype(bf16)
    back = lax.dot_general(
        upstream, adapter_up_weight, (((1,), (1,)), ((), ())), preferred_element_type=f32
    ).astype(bf16)
    user_hot = (
        token_user_slot[:, None] == jnp.arange(ADAPTER_RANK, dtype=jnp.int32)[None, :]
    ).astype(bf16)
    pair = jnp.concatenate([low, back, user_hot], axis=1)
    send_pair = jnp.dot(dispatch, pair, preferred_element_type=f32).astype(bf16)
    got_pair = lax.all_to_all(
        send_pair.reshape(n_data, SLOT, -1), DP, 0, 0, tiled=True
    ).reshape(slots_all, -1)

    rows_hidden = jnp.concatenate([hidden, got_rows[:, :units]], axis=0)
    rows_grad = jnp.concatenate([own_cols, got_rows[:, units:]], axis=0)
    rows_low = jnp.concatenate([low, got_pair[:, :ADAPTER_RANK]], axis=0)
    rows_back = jnp.concatenate([back, got_pair[:, ADAPTER_RANK : 2 * ADAPTER_RANK]], axis=0)
    member = jnp.concatenate(
        [
            user_hot[:, :U_DEV].astype(f32) * local_live[:, None],
            got_pair[:, 2 * ADAPTER_RANK : 2 * ADAPTER_RANK + U_DEV].astype(f32),
        ],
        axis=0,
    )
    same_user = jnp.dot(
        member.astype(bf16), member.astype(bf16).T, preferred_element_type=f32
    )
    pair_part = same_user * (
        row_gram(rows_hidden) * row_gram(rows_back) + row_gram(rows_low) * row_gram(rows_grad)
    )
    norm_part = jnp.sum(member * jnp.sum(pair_part, axis=1)[:, None], axis=0)
    norm_sq = tensor_sum(jnp.pad(norm_part, (0, ADAPTER_RANK - U_DEV))[None, :])[0, :U_DEV]
    factor = clip_norm / jnp.maximum(jnp.sqrt(norm_sq), clip_norm)
    weight = jnp.sum(member * factor[None, :], axis=1) / total_users

    scaled_back = (weight[:, None] * rows_back.astype(f32)).astype(bf16)
    scaled_up = (weight[:, None] * rows_grad.astype(f32)).astype(bf16)
    a_part = column_term(rows_hidden, scaled_back).reshape(N_Y * N_Z, N_CORE, -1, ADAPTER_RANK)
    b_part = column_term(scaled_up, rows_low).reshape(N_Y * N_Z, N_CORE, -1, ADAPTER_RANK)
    both = jnp.concatenate([a_part, b_part], axis=2)
    mine = lax.dynamic_index_in_dim(both, core_index, 1, keepdims=False)
    other = lax.dynamic_index_in_dim(both, 1 - core_index, 1, keepdims=False)
    chip_sum = mine + lax.ppermute(other, "core", [(0, 1), (1, 0)])
    shares = lax.all_to_all(chip_sum.astype(bf16), ("y", "z"), 0, 0, tiled=True)
    total = jnp.sum(shares.astype(f32), axis=0)
    a_rows = units // n_data
    return (total[None, :a_rows], total[None, a_rows:])


def solution(mesh):
    fine = Mesh(
        mesh.devices.reshape(N_Y, N_Z, N_CORE, N_TENSOR), ("y", "z", "core", "tensor")
    )
    in_specs = (
        P(DP, "tensor"),
        P(DP, None),
        P("tensor", None),
        P(),
        P(DP),
        P(DP),
        P(DP, None),
        P(DP, None),
    )
    out_specs = (P("tensor", DP, None), P("tensor", DP, None))
    return jax.shard_map(
        per_device, mesh=fine, in_specs=in_specs, out_specs=out_specs, check_vma=False
    )
```

```python
import functools
import math

import jax
import jax.numpy as jnp
from jax import lax
from jax.experimental import pallas as pl
from jax.experimental.pallas import tpu as pltpu
from jax.sharding import Mesh, PartitionSpec as P

MODEL_WIDTH = 8192
HIDDEN_UNITS = 14336
RANK = 128
U_DEV = 8
SLOT = 2
CLIP_FACTOR = 4.0
N_Y = 4
N_Z = 8
N_CORE = 2
N_TENSOR = 4
N_DATA = N_Y * N_Z * N_CORE
TOK = 256
FAR = N_DATA * SLOT
FOLD = 4
UNITS = HIDDEN_UNITS // N_TENSOR
COLS = MODEL_WIDTH // N_TENSOR
UNITS_Q = UNITS // FOLD
COLS_Q = COLS // FOLD
DP = ("y", "z", "core")
f32 = jnp.float32
bf16 = jnp.bfloat16
i32 = jnp.int32
VMEM = pl.BlockSpec(memory_space=pltpu.VMEM)
SMEM = pl.BlockSpec(memory_space=pltpu.SMEM)


def widths(total):
    return [(at, min(256, total - at)) for at in range(0, total, 256)]


WIDE = pltpu.CompilerParams(vmem_limit_bytes=60 * 1024 * 1024)
NARROW = pltpu.CompilerParams(vmem_limit_bytes=20 * 1024 * 1024)
WIDTH = UNITS_Q + COLS_Q + RANK
CHUNKS = [(0, 0, UNITS_Q, at, width) for at, width in widths(UNITS_Q)] + [
    (1, UNITS_Q, COLS_Q, at, width) for at, width in widths(COLS_Q)
]
HBM = pl.BlockSpec(memory_space=pltpu.HBM)


def cross(left, right):
    return lax.dot_general(left, right, (((1,), (1,)), ((), ())), preferred_element_type=f32)


def dot(left, right):
    return jnp.dot(left, right, preferred_element_type=f32)


def iota(shape, axis):
    return lax.broadcasted_iota(i32, shape, axis)


def picks(slot, parts):
    place = jnp.where(slot < 0, -1, iota((FAR * FOLD, TOK), 0) - slot * FOLD)
    return jnp.concatenate(
        [jnp.where(place == q, 1.0, 0.0).astype(bf16) for q in range(parts)], axis=1
    )


def as_column(row):
    size = row.shape[1]
    eye = iota((size, size), 0) == iota((size, size), 1)
    return jnp.sum(jnp.where(eye, row, 0), axis=1, keepdims=True)


def dispatch_kernel(
    tensor_ref,
    rows_ref,
    home_ref,
    mask_ref,
    user_ref,
    hidden_hbm,
    upstream_hbm,
    send_hbm,
    member_ref,
    hidden_ref,
    cols_ref,
    send_ref,
    in_sem,
    sem,
):
    def arrive(i):
        which, _, part, at, width = CHUNKS[i]
        copies = []
        for q in range(FOLD):
            start = q * part + at
            if which == 0:
                source = hidden_hbm.at[:, start : start + width]
            else:
                own = pl.ds(pl.multiple_of(tensor_ref[0] * COLS + start, RANK), width)
                source = upstream_hbm.at[:, own]
            target = (hidden_ref, cols_ref)[which].at[:, start : start + width]
            copies.append(pltpu.make_async_copy(source, target, in_sem.at[i, q]))
        return copies

    for i in range(len(CHUNKS)):
        for copy in arrive(i):
            copy.start()
    spill = rows_ref.shape[1]
    home = home_ref[...]
    earlier = (as_column(home) == home) & (iota((spill, spill), 0) < iota((spill, spill), 1))
    slot_of = home * SLOT + jnp.sum(earlier.astype(i32), axis=0, keepdims=True)
    hit = as_column(rows_ref[...]) == iota((spill, TOK), 1)
    slot = jnp.sum(jnp.where(hit, as_column(slot_of) + 1, 0), axis=0, keepdims=True) - 1
    real = mask_ref[...] > 0
    pick = picks(jnp.where(real, slot, -1), FOLD)
    user = jnp.where(as_column(user_ref[...]) == iota((TOK, RANK), 1), 1.0, 0.0)
    leave = []

    def put(where, value):
        send_ref[:, where] = value.astype(bf16)
        leave.append(
            pltpu.make_async_copy(send_ref.at[:, where], send_hbm.at[:, where], sem.at[len(leave)])
        )
        leave[-1].start()

    put(slice(WIDTH - RANK, WIDTH), dot(pick[:, :TOK], user.astype(bf16)))
    for i, (which, base, part, at, width) in enumerate(CHUNKS):
        for copy in arrive(i):
            copy.wait()
        ref = (hidden_ref, cols_ref)[which]
        stacked = jnp.concatenate(
            [ref[:, q * part + at : q * part + at + width] for q in range(FOLD)], axis=0
        )
        put(slice(base + at, base + at + width), dot(pick, stacked))
    live = as_column(jnp.where(real & (slot < 0), 1.0, 0.0))
    member_ref[...] = (user * live).astype(bf16)
    for copy in leave:
        copy.wait()


def unfold_kernel(
    got_hbm,
    down_ref,
    up_ref,
    part_ref,
    far_hidden_ref,
    far_cols_ref,
    far_hidden_t_ref,
    far_cols_t_ref,
    far_member_ref,
    got_ref,
    sem,
):
    wheres = [slice(base + at, base + at + width) for _, base, _, at, width in CHUNKS]
    wheres.append(slice(WIDTH - RANK, WIDTH))
    arrive = [
        pltpu.make_async_copy(got_hbm.at[:, where], got_ref.at[:, where], sem.at[i])
        for i, where in enumerate(wheres)
    ]
    for copy in arrive:
        copy.start()
    index = iota((FAR * FOLD, FAR * FOLD), 0)
    want = (index & (FAR - 1)) * FOLD + index // FAR
    pick = jnp.where(iota((FAR * FOLD, FAR * FOLD), 1) == want, 1.0, 0.0).astype(bf16)
    low, back = jnp.zeros((FAR, RANK), f32), jnp.zeros((FAR, RANK), f32)
    for i, (which, base, part, at, width) in enumerate(CHUNKS):
        arrive[i].wait()
        rows = dot(pick, got_ref[:, wheres[i]]).astype(bf16)
        out_ref = (far_hidden_ref, far_cols_ref)[which]
        turned_ref = (far_hidden_t_ref, far_cols_t_ref)[which]
        for q in range(FOLD):
            block = rows[q * FAR : (q + 1) * FAR]
            where = slice(q * part + at, q * part + at + width)
            out_ref[:, where] = block
            turned_ref[where, :] = block.T
            if which == 0:
                low += dot(block, down_ref[where, :])
            else:
                back += cross(block, up_ref[:, where])
    part_ref[:, :RANK] = low
    part_ref[:, RANK:] = back
    arrive[-1].wait()
    far_member_ref[...] = dot(pick[:FAR], got_ref[:, wheres[-1]]).astype(bf16)


def gram_kernel(far_hidden_ref, far_cols_ref, hidden_ref, cols_ref, near_ref, far_ref):
    far_hidden, far_cols = far_hidden_ref[...], far_cols_ref[...]
    near_ref[0] = cross(far_hidden, hidden_ref[...])
    near_ref[1] = cross(far_cols, cols_ref[...])
    far_ref[0] = cross(far_hidden, far_hidden)
    far_ref[1] = cross(far_cols, far_cols)


def norm_kernel(
    part_ref,
    first_ref,
    second_ref,
    third_ref,
    near_ref,
    far_ref,
    far_member_ref,
    member_ref,
    low_ref,
    back_ref,
    local_ref,
    norm_ref,
    far_low_ref,
    far_back_ref,
):
    total = (part_ref[...] + first_ref[...] + second_ref[...] + third_ref[...]).astype(bf16)
    far_low, far_back = total[:, :RANK], total[:, RANK:]
    far_low_ref[...] = far_low
    far_back_ref[...] = far_back
    far_member = far_member_ref[...]
    near = cross(far_member, member_ref[...]) * (
        near_ref[0] * cross(far_back, back_ref[...]) + cross(far_low, low_ref[...]) * near_ref[1]
    )
    far = cross(far_member, far_member) * (
        far_ref[0] * cross(far_back, far_back) + cross(far_low, far_low) * far_ref[1]
    )
    sums = 2.0 * jnp.sum(near, axis=1, keepdims=True) + jnp.sum(far, axis=1, keepdims=True)
    norm_ref[...] = local_ref[...] + jnp.sum(far_member.astype(f32) * sums, axis=0, keepdims=True)


def user_sums(member, pair):
    same = cross(member, member)
    sums = jnp.sum(same * pair, axis=1)[:, None]
    return jnp.sum(member.astype(f32) * sums, axis=0)[None, :]


def core_split(turned, core_index):
    blocks = turned.reshape(N_Y * N_Z, N_CORE, -1, turned.shape[1])
    return [
        lax.dynamic_index_in_dim(blocks, core, 1, keepdims=False).reshape(-1, turned.shape[1])
        for core in (core_index, 1 - core_index)
    ]


def from_others(part):
    return [
        lax.ppermute(part, "tensor", [(i, (i + k) % N_TENSOR) for i in range(N_TENSOR)])
        for k in (1, 3, 2)
    ]


def tensor_sum(part):
    for flip in (1, 3):
        part = part + lax.ppermute(part, "tensor", [(i, i ^ flip) for i in range(N_TENSOR)])
    return part


def per_device(
    hidden,
    upstream,
    adapter_down_weight,
    adapter_up_weight,
    token_user_slot,
    padding_token_mask,
    overflow_user_rows,
    overflow_home_index,
):
    tensor_index = lax.axis_index("tensor")[None].astype(i32)
    core_index = lax.axis_index("core")
    total_users = U_DEV * N_DATA
    clip_norm = CLIP_FACTOR * math.sqrt(RANK * (HIDDEN_UNITS + MODEL_WIDTH))

    def shape(*dims, dtype=bf16):
        return jax.ShapeDtypeStruct(dims, dtype)

    send, member = pl.pallas_call(
        dispatch_kernel,
        out_shape=(shape(FAR * FOLD, WIDTH), shape(TOK, RANK)),
        in_specs=[SMEM, VMEM, VMEM, VMEM, VMEM, HBM, HBM],
        out_specs=(HBM, VMEM),
        scratch_shapes=[
            pltpu.VMEM((TOK, UNITS), bf16),
            pltpu.VMEM((TOK, COLS), bf16),
            pltpu.VMEM((FAR * FOLD, WIDTH), bf16),
            pltpu.SemaphoreType.DMA((len(CHUNKS), FOLD)),
            pltpu.SemaphoreType.DMA((len(CHUNKS) + 1,)),
        ],
        compiler_params=WIDE,
        name="dispatch",
    )(
        tensor_index,
        overflow_user_rows,
        overflow_home_index,
        padding_token_mask[None, :],
        token_user_slot[None, :],
        hidden,
        upstream,
    )
    send, held_hidden, held_upstream = lax.optimization_barrier((send, hidden, upstream))
    got = lax.all_to_all(
        send.reshape(N_DATA, SLOT * FOLD, WIDTH), DP, 0, 0, tiled=True
    ).reshape(FAR * FOLD, WIDTH)

    low_part = dot(held_hidden, adapter_down_weight)
    low = sum(from_others(low_part), low_part).astype(bf16)
    back = cross(held_upstream, adapter_up_weight).astype(bf16)
    own_cols = lax.dynamic_slice_in_dim(held_upstream, tensor_index[0] * COLS, COLS, 1)
    own_up = lax.dynamic_slice_in_dim(adapter_up_weight, tensor_index[0] * COLS, COLS, 1)
    pair_local = cross(held_hidden, held_hidden) * cross(back, back) + cross(low, low) * cross(
        own_cols, own_cols
    )
    norm_local = user_sums(member, pair_local)
    hidden_t = core_split(held_hidden.T, core_index)
    cols_t = core_split(own_cols.T, core_index)
    own_up, norm_local, hidden_t, cols_t = lax.optimization_barrier(
        (own_up, norm_local, hidden_t, cols_t)
    )

    far_part, far_hidden, far_cols, far_hidden_t, far_cols_t, far_member = pl.pallas_call(
        unfold_kernel,
        out_shape=(
            shape(FAR, 2 * RANK, dtype=f32),
            shape(FAR, UNITS),
            shape(FAR, COLS),
            shape(UNITS, FAR),
            shape(COLS, FAR),
            shape(FAR, RANK),
        ),
        in_specs=[HBM, VMEM, VMEM],
        out_specs=(VMEM,) * 6,
        scratch_shapes=[
            pltpu.VMEM((FAR * FOLD, WIDTH), bf16),
            pltpu.SemaphoreType.DMA((len(CHUNKS) + 1,)),
        ],
        compiler_params=NARROW,
        name="unfold",
    )(got, adapter_down_weight, own_up)
    other_parts = from_others(far_part)
    near_gram, far_gram = pl.pallas_call(
        gram_kernel,
        out_shape=(shape(2, FAR, TOK, dtype=f32), shape(2, FAR, FAR, dtype=f32)),
        in_specs=[VMEM] * 4,
        out_specs=(VMEM,) * 2,
        compiler_params=NARROW,
        name="grams",
    )(far_hidden, far_cols, hidden, own_cols)
    norm_part, far_low, far_back = pl.pallas_call(
        norm_kernel,
        out_shape=(shape(1, RANK, dtype=f32), shape(FAR, RANK), shape(FAR, RANK)),
        in_specs=[VMEM] * 11,
        out_specs=(VMEM,) * 3,
        compiler_params=NARROW,
        name="norms",
    )(
        far_part,
        *other_parts,
        near_gram,
        far_gram,
        far_member,
        member,
        low,
        back,
        norm_local,
    )
    far_hidden_t = core_split(far_hidden_t, core_index)
    far_cols_t = core_split(far_cols_t, core_index)
    norm_sq = tensor_sum(norm_part)
    factor = clip_norm / jnp.maximum(jnp.sqrt(norm_sq), clip_norm)
    weight = jnp.sum(member.astype(f32) * factor, axis=1) / total_users
    far_weight = jnp.sum(far_member.astype(f32) * factor, axis=1) / total_users
    scaled_back = (weight[:, None] * back.astype(f32)).astype(bf16)
    far_scaled_back = (far_weight[:, None] * far_back.astype(f32)).astype(bf16)

    def gradient(i):
        a_part = dot(hidden_t[i], scaled_back) + dot(far_hidden_t[i], far_scaled_back)
        scaled_up = (weight[None, :] * cols_t[i].astype(f32)).astype(bf16)
        far_scaled_up = (far_weight[None, :] * far_cols_t[i].astype(f32)).astype(bf16)
        b_part = dot(scaled_up, low) + dot(far_scaled_up, far_low)
        return jnp.concatenate(
            [a_part.reshape(N_Y * N_Z, -1, RANK), b_part.reshape(N_Y * N_Z, -1, RANK)], axis=1
        )

    other, mine = gradient(1), gradient(0)
    chip_sum = mine + lax.ppermute(other, "core", [(0, 1), (1, 0)])
    shares = lax.all_to_all(chip_sum.astype(bf16), ("y", "z"), 0, 0, tiled=True)
    total = jnp.sum(shares.astype(f32), axis=0)
    a_rows = UNITS // N_DATA
    return (total[None, :a_rows], total[None, a_rows:])


def solution(mesh):
    fine = Mesh(
        mesh.devices.reshape(N_Y, N_Z, N_CORE, N_TENSOR), ("y", "z", "core", "tensor")
    )
    in_specs = (
        P(DP, "tensor"),
        P(DP, None),
        P("tensor", None),
        P(),
        P(DP),
        P(DP),
        P(DP, None),
        P(DP, None),
    )
    out_specs = (P("tensor", DP, None), P("tensor", DP, None))
    return jax.shard_map(
        per_device, mesh=fine, in_specs=in_specs, out_specs=out_specs, check_vma=False
    )
```

```python
import functools
import math

import jax
import jax.numpy as jnp
from jax import lax
from jax.experimental import pallas as pl
from jax.experimental.pallas import tpu as pltpu
from jax.sharding import Mesh, PartitionSpec as P

MODEL_WIDTH = 8192
HIDDEN_UNITS = 14336
RANK = 128
U_DEV = 8
SLOT = 2
CLIP_FACTOR = 4.0
N_Y = 4
N_Z = 8
N_CORE = 2
N_TENSOR = 4
N_DATA = N_Y * N_Z * N_CORE
TOK = 256
FAR = N_DATA * SLOT
FOLD = 4
UNITS = HIDDEN_UNITS // N_TENSOR
COLS = MODEL_WIDTH // N_TENSOR
UNITS_Q = UNITS // FOLD
COLS_Q = COLS // FOLD
DP = ("y", "z", "core")
f32 = jnp.float32
bf16 = jnp.bfloat16
i32 = jnp.int32
VMEM = pl.BlockSpec(memory_space=pltpu.VMEM)


def widths(total):
    return [(at, min(256, total - at)) for at in range(0, total, 256)]


NARROW = pltpu.CompilerParams(vmem_limit_bytes=20 * 1024 * 1024)
WIDTH = UNITS_Q + COLS_Q + RANK
SPILL = 64
CHUNKS = [(0, 0, UNITS_Q, at, width) for at, width in widths(UNITS_Q)] + [
    (1, UNITS_Q, COLS_Q, at, width) for at, width in widths(COLS_Q)
]


def cross(left, right):
    return lax.dot_general(left, right, (((1,), (1,)), ((), ())), preferred_element_type=f32)


def dot(left, right):
    return jnp.dot(left, right, preferred_element_type=f32)


def iota(shape, axis):
    return lax.broadcasted_iota(i32, shape, axis)


def picks(slot, parts):
    place = jnp.where(slot < 0, -1, iota((FAR * FOLD, TOK), 0) - slot * FOLD)
    return jnp.concatenate(
        [jnp.where(place == q, 1.0, 0.0).astype(bf16) for q in range(parts)], axis=1
    )


def as_column(row):
    size = row.shape[1]
    eye = iota((size, size), 0) == iota((size, size), 1)
    return jnp.sum(jnp.where(eye, row, 0), axis=1, keepdims=True)


def slots_of(home):
    size = home.shape[1]
    earlier = (as_column(home) == home) & (iota((size, size), 0) < iota((size, size), 1))
    return home * SLOT + jnp.sum(earlier.astype(i32), axis=0, keepdims=True)


def lead_kernel(
    rows_ref, mask_ref, user_ref, hidden_ref, cols_ref, down_ref, up_ref, part_ref, hot_ref
):
    listed = as_column(rows_ref[...]) == iota((SPILL, TOK), 1)
    pick = jnp.where(listed & (mask_ref[...] > 0), 1.0, 0.0).astype(bf16)
    user = jnp.where(as_column(user_ref[...]) == iota((TOK, RANK), 1), 1.0, 0.0).astype(bf16)
    hot_ref[...] = dot(pick, user).astype(bf16)
    part_ref[:, :RANK] = dot(dot(pick, hidden_ref[...]).astype(bf16), down_ref[...])
    part_ref[:, RANK:] = cross(dot(pick, cols_ref[...]).astype(bf16), up_ref[...])


def dispatch_kernel(
    rows_ref, home_ref, mask_ref, user_ref, hidden_ref, cols_ref, send_ref, member_ref
):
    slot_of = as_column(slots_of(home_ref[...]))
    hit = as_column(rows_ref[...]) == iota((SPILL, TOK), 1)
    slot = jnp.sum(jnp.where(hit, slot_of + 1, 0), axis=0, keepdims=True) - 1
    real = mask_ref[...] > 0
    pick = picks(jnp.where(real, slot, -1), FOLD)
    for which, base, part, at, width in CHUNKS:
        ref = (hidden_ref, cols_ref)[which]
        stacked = jnp.concatenate(
            [ref[:, q * part + at : q * part + at + width] for q in range(FOLD)], axis=0
        )
        send_ref[:, base + at : base + at + width] = dot(pick, stacked).astype(bf16)
    user = jnp.where(as_column(user_ref[...]) == iota((TOK, RANK), 1), 1.0, 0.0)
    live = as_column(jnp.where(real & (slot < 0), 1.0, 0.0))
    member_ref[...] = (user * live).astype(bf16)


def pair_kernel(
    part_ref, first_ref, second_ref, third_ref, hot_ref, home_ref, out_ref
):
    total = (part_ref[...] + first_ref[...] + second_ref[...] + third_ref[...]).astype(bf16)
    stacked = jnp.concatenate([total[:, :RANK], total[:, RANK:], hot_ref[...]], axis=0)
    place = iota((FAR * FOLD, SPILL), 0) - slots_of(home_ref[...]) * FOLD
    pick = jnp.concatenate([jnp.where(place == p, 1.0, 0.0) for p in range(3)], axis=1)
    out_ref[...] = dot(pick.astype(bf16), stacked).astype(bf16)


def unfold_kernel(got_ref, far_hidden_ref, far_cols_ref, far_low_ref, far_back_ref, far_member_ref):
    index = iota((FAR * FOLD, FAR * FOLD), 0)
    want = (index & (FAR - 1)) * FOLD + index // FAR
    pick = jnp.where(iota((FAR * FOLD, FAR * FOLD), 1) == want, 1.0, 0.0).astype(bf16)
    for which, base, part, at, width in CHUNKS:
        rows = dot(pick, got_ref[:, base + at : base + at + width]).astype(bf16)
        out_ref = (far_hidden_ref, far_cols_ref)[which]
        for q in range(FOLD):
            where = slice(q * part + at, q * part + at + width)
            out_ref[:, where] = rows[q * FAR : (q + 1) * FAR]
    rows = dot(pick, got_ref[:, WIDTH - RANK : WIDTH]).astype(bf16)
    for q, out_ref in enumerate((far_low_ref, far_back_ref, far_member_ref)):
        out_ref[...] = rows[q * FAR : (q + 1) * FAR]


def far_kernel(
    far_hidden_ref,
    far_cols_ref,
    far_low_ref,
    far_back_ref,
    far_member_ref,
    cols_ref,
    low_ref,
    back_ref,
    member_ref,
    near_ref,
    sums_ref,
):
    far_hidden, far_cols = far_hidden_ref[...], far_cols_ref[...]
    far_low, far_back, far_member = far_low_ref[...], far_back_ref[...], far_member_ref[...]
    same = 2.0 * cross(far_member, member_ref[...])
    near_ref[...] = same * cross(far_back, back_ref[...])
    near = same * (cross(far_low, low_ref[...]) * cross(far_cols, cols_ref[...]))
    far = cross(far_member, far_member) * (
        cross(far_hidden, far_hidden) * cross(far_back, far_back)
        + cross(far_low, far_low) * cross(far_cols, far_cols)
    )
    sums = jnp.sum(near, axis=1, keepdims=True) + jnp.sum(far, axis=1, keepdims=True)
    sums_ref[...] = jnp.broadcast_to(sums, sums_ref.shape)


def norm_kernel(
    far_hidden_ref, hidden_ref, near_ref, sums_ref, far_member_ref, local_ref, norm_ref
):
    near = near_ref[...] * cross(far_hidden_ref[...], hidden_ref[...])
    sums = sums_ref[:, :1] + jnp.sum(near, axis=1, keepdims=True)
    far_member = far_member_ref[...].astype(f32)
    norm_ref[...] = local_ref[...] + jnp.sum(far_member * sums, axis=0, keepdims=True)


def finish_kernel(shares_ref, a_ref, b_ref):
    total = jnp.sum(shares_ref[...].astype(f32), axis=0)
    a_ref[0] = total[: UNITS // N_DATA]
    b_ref[0] = total[UNITS // N_DATA :]


def turn_kernel(hidden_ref, cols_ref, hidden_t_ref, cols_t_ref):
    for ref, out_ref in ((hidden_ref, hidden_t_ref), (cols_ref, cols_t_ref)):
        for at in range(0, ref.shape[1], 256):
            out_ref[at : at + 256, :] = ref[:, at : at + 256].T


def user_sums(member, pair):
    same = cross(member, member)
    sums = jnp.sum(same * pair, axis=1)[:, None]
    return jnp.sum(member.astype(f32) * sums, axis=0)[None, :]


def core_split(turned, core_index):
    blocks = turned.reshape(N_Y * N_Z, N_CORE, -1, turned.shape[1])
    return [
        lax.dynamic_index_in_dim(blocks, core, 1, keepdims=False).reshape(-1, turned.shape[1])
        for core in (core_index, 1 - core_index)
    ]


def from_others(part):
    return [
        lax.ppermute(part, "tensor", [(i, (i + k) % N_TENSOR) for i in range(N_TENSOR)])
        for k in (1, 3, 2)
    ]


def tensor_sum(part):
    for flip in (1, 3):
        part = part + lax.ppermute(part, "tensor", [(i, i ^ flip) for i in range(N_TENSOR)])
    return part


def per_device(
    hidden,
    upstream,
    adapter_down_weight,
    adapter_up_weight,
    token_user_slot,
    padding_token_mask,
    overflow_user_rows,
    overflow_home_index,
):
    tensor_index = lax.axis_index("tensor")
    core_index = lax.axis_index("core")
    total_users = U_DEV * N_DATA
    clip_norm = CLIP_FACTOR * math.sqrt(RANK * (HIDDEN_UNITS + MODEL_WIDTH))

    def shape(*dims, dtype=bf16):
        return jax.ShapeDtypeStruct(dims, dtype)

    own = tensor_index * COLS
    own_cols = lax.dynamic_slice_in_dim(upstream, own, COLS, 1)
    own_up = lax.dynamic_slice_in_dim(adapter_up_weight, own, COLS, 1)
    rows, home = overflow_user_rows, overflow_home_index
    mask, user = padding_token_mask[None, :], token_user_slot[None, :]
    part, hot = pl.pallas_call(
        lead_kernel,
        out_shape=(shape(SPILL, 2 * RANK, dtype=f32), shape(SPILL, RANK)),
        in_specs=[VMEM] * 7,
        out_specs=(VMEM,) * 2,
        compiler_params=NARROW,
        name="lead",
    )(rows, mask, user, hidden, own_cols, adapter_down_weight, own_up)
    parts = from_others(part)
    send, member = pl.pallas_call(
        dispatch_kernel,
        out_shape=(shape(FAR * FOLD, UNITS_Q + COLS_Q), shape(TOK, RANK)),
        in_specs=[VMEM] * 6,
        out_specs=(VMEM,) * 2,
        compiler_params=NARROW,
        name="dispatch",
    )(rows, home, mask, user, hidden, own_cols)
    pair = pl.pallas_call(
        pair_kernel,
        out_shape=shape(FAR * FOLD, RANK),
        in_specs=[VMEM] * 6,
        out_specs=VMEM,
        compiler_params=NARROW,
        name="pair",
    )(part, *parts, hot, home)
    send = jnp.concatenate([send, pair], axis=1)
    send, held_hidden, held_upstream, held_cols = lax.optimization_barrier(
        (send, hidden, upstream, own_cols)
    )
    got = lax.all_to_all(
        send.reshape(N_DATA, SLOT * FOLD, WIDTH), DP, 0, 0, tiled=True
    ).reshape(FAR * FOLD, WIDTH)

    low_part = dot(held_hidden, adapter_down_weight)
    low = sum(from_others(low_part), low_part).astype(bf16)
    back = cross(held_upstream, adapter_up_weight).astype(bf16)
    pair_local = cross(held_hidden, held_hidden) * cross(back, back) + cross(low, low) * cross(
        held_cols, held_cols
    )
    norm_local = user_sums(member, pair_local)
    hidden_t = core_split(held_hidden.T, core_index)
    cols_t = core_split(held_cols.T, core_index)
    got, norm_local, hidden_t, cols_t = lax.optimization_barrier(
        (got, norm_local, hidden_t, cols_t)
    )

    far_hidden, far_cols, far_low, far_back, far_member = pl.pallas_call(
        unfold_kernel,
        out_shape=(shape(FAR, UNITS), shape(FAR, COLS)) + (shape(FAR, RANK),) * 3,
        in_specs=[VMEM],
        out_specs=(VMEM,) * 5,
        compiler_params=NARROW,
        name="unfold",
    )(got)
    near, sums = pl.pallas_call(
        far_kernel,
        out_shape=(shape(FAR, TOK, dtype=f32), shape(FAR, RANK, dtype=f32)),
        in_specs=[VMEM] * 9,
        out_specs=(VMEM,) * 2,
        compiler_params=NARROW,
        name="far",
    )(far_hidden, far_cols, far_low, far_back, far_member, own_cols, low, back, member)
    norm_part = pl.pallas_call(
        norm_kernel,
        out_shape=shape(1, RANK, dtype=f32),
        in_specs=[VMEM] * 6,
        out_specs=VMEM,
        compiler_params=NARROW,
        name="norms",
    )(far_hidden, hidden, near, sums, far_member, norm_local)
    norm_part, far_hidden, far_cols = lax.optimization_barrier((norm_part, far_hidden, far_cols))
    far_hidden_t, far_cols_t = pl.pallas_call(
        turn_kernel,
        out_shape=(shape(UNITS, FAR), shape(COLS, FAR)),
        in_specs=[VMEM] * 2,
        out_specs=(VMEM,) * 2,
        compiler_params=NARROW,
        name="turn",
    )(far_hidden, far_cols)
    far_hidden_t = core_split(far_hidden_t, core_index)
    far_cols_t = core_split(far_cols_t, core_index)
    norm_sq = tensor_sum(norm_part)
    factor = clip_norm / jnp.maximum(jnp.sqrt(norm_sq), clip_norm)
    weight = jnp.sum(member.astype(f32) * factor, axis=1) / total_users
    far_weight = jnp.sum(far_member.astype(f32) * factor, axis=1) / total_users
    scaled_back = (weight[:, None] * back.astype(f32)).astype(bf16)
    far_scaled_back = (far_weight[:, None] * far_back.astype(f32)).astype(bf16)

    def gradient(i):
        a_part = dot(hidden_t[i], scaled_back) + dot(far_hidden_t[i], far_scaled_back)
        scaled_up = (weight[None, :] * cols_t[i].astype(f32)).astype(bf16)
        far_scaled_up = (far_weight[None, :] * far_cols_t[i].astype(f32)).astype(bf16)
        b_part = dot(scaled_up, low) + dot(far_scaled_up, far_low)
        return jnp.concatenate(
            [a_part.reshape(N_Y * N_Z, -1, RANK), b_part.reshape(N_Y * N_Z, -1, RANK)], axis=1
        )

    other, mine = gradient(1), gradient(0)
    chip_sum = mine + lax.ppermute(other, "core", [(0, 1), (1, 0)])
    shares = lax.all_to_all(chip_sum.astype(bf16), ("y", "z"), 0, 0, tiled=True)
    return pl.pallas_call(
        finish_kernel,
        out_shape=(
            shape(1, UNITS // N_DATA, RANK, dtype=f32),
            shape(1, COLS // N_DATA, RANK, dtype=f32),
        ),
        in_specs=[VMEM],
        out_specs=(VMEM,) * 2,
        compiler_params=NARROW,
        name="finish",
    )(shares)


def solution(mesh):
    fine = Mesh(
        mesh.devices.reshape(N_Y, N_Z, N_CORE, N_TENSOR), ("y", "z", "core", "tensor")
    )
    in_specs = (
        P(DP, "tensor"),
        P(DP, None),
        P("tensor", None),
        P(),
        P(DP),
        P(DP),
        P(DP, None),
        P(DP, None),
    )
    out_specs = (P("tensor", DP, None), P("tensor", DP, None))
    return jax.shard_map(
        per_device, mesh=fine, in_specs=in_specs, out_specs=out_specs, check_vma=False
    )
```

```python
import functools
import math

import jax
import jax.numpy as jnp
from jax import lax
from jax.experimental import pallas as pl
from jax.experimental.pallas import tpu as pltpu
from jax.sharding import Mesh, PartitionSpec as P

MODEL_WIDTH = 8192
HIDDEN_UNITS = 14336
RANK = 128
U_DEV = 8
SLOT = 2
CLIP_FACTOR = 4.0
N_Y = 4
N_Z = 8
N_CORE = 2
N_TENSOR = 4
N_DATA = N_Y * N_Z * N_CORE
TOK = 256
FAR = N_DATA * SLOT
FOLD = 4
UNITS = HIDDEN_UNITS // N_TENSOR
COLS = MODEL_WIDTH // N_TENSOR
UNITS_Q = UNITS // FOLD
COLS_Q = COLS // FOLD
DP = ("y", "z", "core")
f32 = jnp.float32
bf16 = jnp.bfloat16
i32 = jnp.int32
VMEM = pl.BlockSpec(memory_space=pltpu.VMEM)
HBM = pl.BlockSpec(memory_space=pltpu.HBM)


def widths(total):
    return [(at, min(256, total - at)) for at in range(0, total, 256)]


NARROW = pltpu.CompilerParams(vmem_limit_bytes=20 * 1024 * 1024)
WIDTH = UNITS_Q + COLS_Q + RANK
SPILL = 64
UNFOLD = 128
CHUNKS = [(0, 0, UNITS_Q, at, width) for at, width in widths(UNITS_Q)] + [
    (1, UNITS_Q, COLS_Q, at, width) for at, width in widths(COLS_Q)
]


def cross(left, right):
    return lax.dot_general(left, right, (((1,), (1,)), ((), ())), preferred_element_type=f32)


def dot(left, right):
    return jnp.dot(left, right, preferred_element_type=f32)


def iota(shape, axis):
    return lax.broadcasted_iota(i32, shape, axis)


def picks(slot, parts):
    place = jnp.where(slot < 0, -1, iota((FAR * FOLD, TOK), 0) - slot * FOLD)
    return jnp.concatenate(
        [jnp.where(place == q, 1.0, 0.0).astype(bf16) for q in range(parts)], axis=1
    )


def as_column(row):
    size = row.shape[1]
    eye = iota((size, size), 0) == iota((size, size), 1)
    return jnp.sum(jnp.where(eye, row, 0), axis=1, keepdims=True)


def slots_of(home):
    size = home.shape[1]
    earlier = (as_column(home) == home) & (iota((size, size), 0) < iota((size, size), 1))
    return home * SLOT + jnp.sum(earlier.astype(i32), axis=0, keepdims=True)


def lead_kernel(
    rows_ref, mask_ref, user_ref, hidden_ref, cols_ref, down_ref, up_ref, part_ref, hot_ref
):
    listed = as_column(rows_ref[...]) == iota((SPILL, TOK), 1)
    pick = jnp.where(listed & (mask_ref[...] > 0), 1.0, 0.0).astype(bf16)
    user = jnp.where(as_column(user_ref[...]) == iota((TOK, RANK), 1), 1.0, 0.0).astype(bf16)
    hot_ref[...] = dot(pick, user).astype(bf16)
    part_ref[:, :RANK] = dot(dot(pick, hidden_ref[...]).astype(bf16), down_ref[...])
    part_ref[:, RANK:] = cross(dot(pick, cols_ref[...]).astype(bf16), up_ref[...])


def dispatch_kernel(
    rows_ref, home_ref, mask_ref, user_ref, hidden_ref, cols_ref, send_ref, member_ref
):
    slot_of = as_column(slots_of(home_ref[...]))
    hit = as_column(rows_ref[...]) == iota((SPILL, TOK), 1)
    slot = jnp.sum(jnp.where(hit, slot_of + 1, 0), axis=0, keepdims=True) - 1
    real = mask_ref[...] > 0
    pick = picks(jnp.where(real, slot, -1), FOLD)
    for which, base, part, at, width in CHUNKS:
        ref = (hidden_ref, cols_ref)[which]
        stacked = jnp.concatenate(
            [ref[:, q * part + at : q * part + at + width] for q in range(FOLD)], axis=0
        )
        send_ref[:, base + at : base + at + width] = dot(pick, stacked).astype(bf16)
    user = jnp.where(as_column(user_ref[...]) == iota((TOK, RANK), 1), 1.0, 0.0)
    live = as_column(jnp.where(real & (slot < 0), 1.0, 0.0))
    member_ref[...] = (user * live).astype(bf16)


def pair_kernel(part_ref, first_ref, second_ref, third_ref, hot_ref, home_ref, out_ref):
    total = (part_ref[...] + first_ref[...] + second_ref[...] + third_ref[...]).astype(bf16)
    stacked = jnp.concatenate([total[:, :RANK], total[:, RANK:], hot_ref[...]], axis=0)
    place = iota((FAR * FOLD, SPILL), 0) - slots_of(home_ref[...]) * FOLD
    pick = jnp.concatenate([jnp.where(place == p, 1.0, 0.0) for p in range(3)], axis=1)
    out_ref[...] = dot(pick.astype(bf16), stacked).astype(bf16)


def unfold_kernel(
    got_hbm, far_hidden_ref, far_cols_ref, far_low_ref, far_back_ref, far_member_ref, got_ref, sem
):
    arrive = []
    for i in range(FAR * FOLD // UNFOLD):
        rows = pl.ds(i * UNFOLD, UNFOLD)
        arrive.append(pltpu.make_async_copy(got_hbm.at[rows, :], got_ref.at[rows, :], sem.at[i]))
    for copy in arrive:
        copy.start()
    size = UNFOLD // FOLD
    index = iota((UNFOLD, UNFOLD), 0)
    want = index % size * FOLD + index // size
    pick = jnp.where(iota((UNFOLD, UNFOLD), 1) == want, 1.0, 0.0).astype(bf16)
    for i, copy in enumerate(arrive):
        copy.wait()
        to = slice(i * size, (i + 1) * size)
        block = got_ref[i * UNFOLD : (i + 1) * UNFOLD, :]
        for which, base, part, at, width in CHUNKS:
            rows = dot(pick, block[:, base + at : base + at + width]).astype(bf16)
            out_ref = (far_hidden_ref, far_cols_ref)[which]
            for q in range(FOLD):
                where = slice(q * part + at, q * part + at + width)
                out_ref[to, where] = rows[q * size : (q + 1) * size]
        rows = dot(pick, block[:, WIDTH - RANK : WIDTH]).astype(bf16)
        for q, out_ref in enumerate((far_low_ref, far_back_ref, far_member_ref)):
            out_ref[to, :] = rows[q * size : (q + 1) * size]


def far_kernel(
    far_hidden_ref,
    far_cols_ref,
    far_low_ref,
    far_back_ref,
    far_member_ref,
    cols_ref,
    low_ref,
    back_ref,
    member_ref,
    near_ref,
    sums_ref,
):
    far_hidden, far_cols = far_hidden_ref[...], far_cols_ref[...]
    far_low, far_back, far_member = far_low_ref[...], far_back_ref[...], far_member_ref[...]
    same = 2.0 * cross(far_member, member_ref[...])
    near_ref[...] = same * cross(far_back, back_ref[...])
    near = same * (cross(far_low, low_ref[...]) * cross(far_cols, cols_ref[...]))
    far = cross(far_member, far_member) * (
        cross(far_hidden, far_hidden) * cross(far_back, far_back)
        + cross(far_low, far_low) * cross(far_cols, far_cols)
    )
    sums = jnp.sum(near, axis=1, keepdims=True) + jnp.sum(far, axis=1, keepdims=True)
    sums_ref[...] = jnp.broadcast_to(sums, sums_ref.shape)


def norm_kernel(
    far_hidden_ref, hidden_ref, near_ref, sums_ref, far_member_ref, local_ref, norm_ref
):
    near = near_ref[...] * cross(far_hidden_ref[...], hidden_ref[...])
    sums = sums_ref[:, :1] + jnp.sum(near, axis=1, keepdims=True)
    far_member = far_member_ref[...].astype(f32)
    norm_ref[...] = local_ref[...] + jnp.sum(far_member * sums, axis=0, keepdims=True)


def finish_kernel(shares_ref, a_ref, b_ref):
    total = jnp.sum(shares_ref[...].astype(f32), axis=0)
    a_ref[0] = total[: UNITS // N_DATA]
    b_ref[0] = total[UNITS // N_DATA :]


def turn_kernel(hidden_ref, cols_ref, hidden_t_ref, cols_t_ref):
    for ref, out_ref in ((hidden_ref, hidden_t_ref), (cols_ref, cols_t_ref)):
        for at in range(0, ref.shape[1], 256):
            out_ref[at : at + 256, :] = ref[:, at : at + 256].T


def user_sums(member, pair):
    same = cross(member, member)
    sums = jnp.sum(same * pair, axis=1)[:, None]
    return jnp.sum(member.astype(f32) * sums, axis=0)[None, :]


def core_split(turned, core_index):
    blocks = turned.reshape(N_Y * N_Z, N_CORE, -1, turned.shape[1])
    return [
        lax.dynamic_index_in_dim(blocks, core, 1, keepdims=False).reshape(-1, turned.shape[1])
        for core in (core_index, 1 - core_index)
    ]


def from_others(part):
    return [
        lax.ppermute(part, "tensor", [(i, (i + k) % N_TENSOR) for i in range(N_TENSOR)])
        for k in (1, 3, 2)
    ]


def flip_tensor(part, flip):
    return lax.ppermute(part, "tensor", [(i, i ^ flip) for i in range(N_TENSOR)])


def per_device(
    hidden,
    upstream,
    adapter_down_weight,
    adapter_up_weight,
    token_user_slot,
    padding_token_mask,
    overflow_user_rows,
    overflow_home_index,
):
    tensor_index = lax.axis_index("tensor")
    core_index = lax.axis_index("core")
    total_users = U_DEV * N_DATA
    clip_norm = CLIP_FACTOR * math.sqrt(RANK * (HIDDEN_UNITS + MODEL_WIDTH))

    def shape(*dims, dtype=bf16):
        return jax.ShapeDtypeStruct(dims, dtype)

    own = tensor_index * COLS
    own_cols = lax.dynamic_slice_in_dim(upstream, own, COLS, 1)
    own_up = lax.dynamic_slice_in_dim(adapter_up_weight, own, COLS, 1)
    rows, home = overflow_user_rows, overflow_home_index
    mask, user = padding_token_mask[None, :], token_user_slot[None, :]
    part, hot = pl.pallas_call(
        lead_kernel,
        out_shape=(shape(SPILL, 2 * RANK, dtype=f32), shape(SPILL, RANK)),
        in_specs=[VMEM] * 7,
        out_specs=(VMEM,) * 2,
        compiler_params=NARROW,
        name="lead",
    )(rows, mask, user, hidden, own_cols, adapter_down_weight, own_up)
    parts = from_others(part)
    send, member = pl.pallas_call(
        dispatch_kernel,
        out_shape=(shape(FAR * FOLD, UNITS_Q + COLS_Q), shape(TOK, RANK)),
        in_specs=[VMEM] * 6,
        out_specs=(VMEM,) * 2,
        compiler_params=NARROW,
        name="dispatch",
    )(rows, home, mask, user, hidden, own_cols)
    pair = pl.pallas_call(
        pair_kernel,
        out_shape=shape(FAR * FOLD, RANK),
        in_specs=[VMEM] * 6,
        out_specs=VMEM,
        compiler_params=NARROW,
        name="pair",
    )(part, *parts, hot, home)
    send = jnp.concatenate([send, pair], axis=1)
    send, held_hidden, held_upstream, held_cols = lax.optimization_barrier(
        (send, hidden, upstream, own_cols)
    )
    got = lax.all_to_all(
        send.reshape(N_DATA, SLOT * FOLD, WIDTH), DP, 0, 0, tiled=True
    ).reshape(FAR * FOLD, WIDTH)

    low_part = dot(held_hidden, adapter_down_weight)
    low = sum(from_others(low_part), low_part).astype(bf16)
    back = cross(held_upstream, adapter_up_weight).astype(bf16)
    pair_local = cross(held_hidden, held_hidden) * cross(back, back) + cross(low, low) * cross(
        held_cols, held_cols
    )
    norm_local = user_sums(member, pair_local)
    hidden_t = core_split(held_hidden.T, core_index)
    cols_t = core_split(held_cols.T, core_index)
    got, norm_local, hidden_t, cols_t = lax.optimization_barrier(
        (got, norm_local, hidden_t, cols_t)
    )

    far_hidden, far_cols, far_low, far_back, far_member = pl.pallas_call(
        unfold_kernel,
        out_shape=(shape(FAR, UNITS), shape(FAR, COLS)) + (shape(FAR, RANK),) * 3,
        in_specs=[HBM],
        out_specs=(VMEM,) * 5,
        scratch_shapes=[
            pltpu.VMEM((FAR * FOLD, WIDTH), bf16),
            pltpu.SemaphoreType.DMA((FAR * FOLD // UNFOLD,)),
        ],
        compiler_params=NARROW,
        name="unfold",
    )(got)
    near, sums = pl.pallas_call(
        far_kernel,
        out_shape=(shape(FAR, TOK, dtype=f32), shape(FAR, RANK, dtype=f32)),
        in_specs=[VMEM] * 9,
        out_specs=(VMEM,) * 2,
        compiler_params=NARROW,
        name="far",
    )(far_hidden, far_cols, far_low, far_back, far_member, own_cols, low, back, member)
    norm_part = pl.pallas_call(
        norm_kernel,
        out_shape=shape(1, RANK, dtype=f32),
        in_specs=[VMEM] * 6,
        out_specs=VMEM,
        compiler_params=NARROW,
        name="norms",
    )(far_hidden, hidden, near, sums, far_member, norm_local)
    norm_part, far_hidden, far_cols = lax.optimization_barrier((norm_part, far_hidden, far_cols))
    far_hidden_t, far_cols_t = pl.pallas_call(
        turn_kernel,
        out_shape=(shape(UNITS, FAR), shape(COLS, FAR)),
        in_specs=[VMEM] * 2,
        out_specs=(VMEM,) * 2,
        compiler_params=NARROW,
        name="turn",
    )(far_hidden, far_cols)
    far_hidden_t = core_split(far_hidden_t, core_index)
    far_cols_t = core_split(far_cols_t, core_index)
    norm_part = norm_part + flip_tensor(norm_part, 1)
    norm_sq = norm_part + flip_tensor(norm_part, 3)
    factor = clip_norm / jnp.maximum(jnp.sqrt(norm_sq), clip_norm)
    weight = jnp.sum(member.astype(f32) * factor, axis=1) / total_users
    far_weight = jnp.sum(far_member.astype(f32) * factor, axis=1) / total_users
    scaled_back = (weight[:, None] * back.astype(f32)).astype(bf16)
    far_scaled_back = (far_weight[:, None] * far_back.astype(f32)).astype(bf16)

    def a_blocks(i, scaled_back):
        total = dot(hidden_t[i], scaled_back) + dot(far_hidden_t[i], far_scaled_back)
        return total.reshape(N_Y * N_Z, -1, RANK)

    def b_blocks(i, low):
        scaled_up = (weight[None, :] * cols_t[i].astype(f32)).astype(bf16)
        far_scaled_up = (far_weight[None, :] * far_cols_t[i].astype(f32)).astype(bf16)
        total = dot(scaled_up, low) + dot(far_scaled_up, far_low)
        return total.reshape(N_Y * N_Z, -1, RANK)

    def from_core(blocks):
        return lax.ppermute(blocks, "core", [(0, 1), (1, 0)])

    other_b = b_blocks(1, low)
    come_b = from_core(other_b)
    held_back, other_b = lax.optimization_barrier((scaled_back, other_b))
    other_a = a_blocks(1, held_back)
    come_a = from_core(other_a)
    held_back, held_low, other_a = lax.optimization_barrier((scaled_back, low, other_a))
    chip_sum = jnp.concatenate(
        [a_blocks(0, held_back) + come_a, b_blocks(0, held_low) + come_b], axis=1
    )
    shares = lax.all_to_all(chip_sum.astype(bf16), ("y", "z"), 0, 0, tiled=True)
    return pl.pallas_call(
        finish_kernel,
        out_shape=(
            shape(1, UNITS // N_DATA, RANK, dtype=f32),
            shape(1, COLS // N_DATA, RANK, dtype=f32),
        ),
        in_specs=[VMEM],
        out_specs=(VMEM,) * 2,
        compiler_params=NARROW,
        name="finish",
    )(shares)


def solution(mesh):
    fine = Mesh(
        mesh.devices.reshape(N_Y, N_Z, N_CORE, N_TENSOR), ("y", "z", "core", "tensor")
    )
    in_specs = (
        P(DP, "tensor"),
        P(DP, None),
        P("tensor", None),
        P(),
        P(DP),
        P(DP),
        P(DP, None),
        P(DP, None),
    )
    out_specs = (P("tensor", DP, None), P("tensor", DP, None))
    return jax.shard_map(
        per_device, mesh=fine, in_specs=in_specs, out_specs=out_specs, check_vma=False
    )
```

```python
import functools
import math

import jax
import jax.numpy as jnp
from jax import lax
from jax.experimental import pallas as pl
from jax.experimental.pallas import tpu as pltpu
from jax.sharding import Mesh, PartitionSpec as P

MODEL_WIDTH = 8192
HIDDEN_UNITS = 14336
RANK = 128
U_DEV = 8
SLOT = 2
CLIP_FACTOR = 4.0
N_Y = 4
N_Z = 8
N_CORE = 2
N_TENSOR = 4
N_DATA = N_Y * N_Z * N_CORE
TOK = 256
FAR = N_DATA * SLOT
FOLD = 4
UNITS = HIDDEN_UNITS // N_TENSOR
COLS = MODEL_WIDTH // N_TENSOR
UNITS_Q = UNITS // FOLD
COLS_Q = COLS // FOLD
DP = ("y", "z", "core")
f32 = jnp.float32
bf16 = jnp.bfloat16
i32 = jnp.int32
VMEM = pl.BlockSpec(memory_space=pltpu.VMEM)
HBM = pl.BlockSpec(memory_space=pltpu.HBM)


def widths(total):
    return [(at, min(256, total - at)) for at in range(0, total, 256)]


NARROW = pltpu.CompilerParams(vmem_limit_bytes=20 * 1024 * 1024)
WIDTH = UNITS_Q + COLS_Q + RANK
SPILL = 64
UNFOLD = 128
CHUNKS = [(0, 0, UNITS_Q, at, width) for at, width in widths(UNITS_Q)] + [
    (1, UNITS_Q, COLS_Q, at, width) for at, width in widths(COLS_Q)
]


def cross(left, right):
    return lax.dot_general(left, right, (((1,), (1,)), ((), ())), preferred_element_type=f32)


def dot(left, right):
    return jnp.dot(left, right, preferred_element_type=f32)


def iota(shape, axis):
    return lax.broadcasted_iota(i32, shape, axis)


def as_column(row):
    size = row.shape[1]
    eye = iota((size, size), 0) == iota((size, size), 1)
    return jnp.sum(jnp.where(eye, row, 0), axis=1, keepdims=True)


def slots_of(home):
    size = home.shape[1]
    earlier = (as_column(home) == home) & (iota((size, size), 0) < iota((size, size), 1))
    return home * SLOT + jnp.sum(earlier.astype(i32), axis=0, keepdims=True)


def lead_kernel(
    rows_ref, mask_ref, user_ref, hidden_ref, cols_ref, down_ref, up_ref, part_ref, hot_ref
):
    listed = as_column(rows_ref[...]) == iota((SPILL, TOK), 1)
    pick = jnp.where(listed & (mask_ref[...] > 0), 1.0, 0.0).astype(bf16)
    user = jnp.where(as_column(user_ref[...]) == iota((TOK, RANK), 1), 1.0, 0.0).astype(bf16)
    hot_ref[...] = dot(pick, user).astype(bf16)
    part_ref[:, :RANK] = dot(dot(pick, hidden_ref[...]).astype(bf16), down_ref[...])
    part_ref[:, RANK:] = cross(dot(pick, cols_ref[...]).astype(bf16), up_ref[...])


def dispatch_kernel(
    rows_ref, home_ref, mask_ref, user_ref, hidden_ref, cols_ref, send_ref, member_ref, wide_ref
):
    slot_of = as_column(slots_of(home_ref[...]))
    hit = as_column(rows_ref[...]) == iota((SPILL, TOK), 1)
    slot = jnp.sum(jnp.where(hit, slot_of + 1, 0), axis=0, keepdims=True) - 1
    real = mask_ref[...] > 0
    pick = jnp.where(iota((FAR, TOK), 0) == jnp.where(real, slot, -1), 1.0, 0.0).astype(bf16)
    for which, base, part, at, width in CHUNKS:
        ref = (hidden_ref, cols_ref)[which]
        for q in range(FOLD):
            rows = dot(pick, ref[:, q * part + at : q * part + at + width])
            for lane in range(0, width, RANK):
                tile = (base + at + lane) // RANK
                wide_ref[tile, pl.ds(q, FAR, stride=FOLD), :] = rows[:, lane : lane + RANK]
        for lane in range(base + at, base + at + width, RANK):
            send_ref[:, lane : lane + RANK] = wide_ref[lane // RANK].astype(bf16)
    user = jnp.where(as_column(user_ref[...]) == iota((TOK, RANK), 1), 1.0, 0.0)
    live = as_column(jnp.where(real & (slot < 0), 1.0, 0.0))
    member_ref[...] = (user * live).astype(bf16)


def pair_kernel(part_ref, first_ref, second_ref, third_ref, hot_ref, home_ref, out_ref):
    total = (part_ref[...] + first_ref[...] + second_ref[...] + third_ref[...]).astype(bf16)
    stacked = jnp.concatenate([total[:, :RANK], total[:, RANK:], hot_ref[...]], axis=0)
    place = iota((FAR * FOLD, SPILL), 0) - slots_of(home_ref[...]) * FOLD
    pick = jnp.concatenate([jnp.where(place == p, 1.0, 0.0) for p in range(3)], axis=1)
    out_ref[...] = dot(pick.astype(bf16), stacked).astype(bf16)


def unfold_kernel(
    got_hbm, far_hidden_ref, far_cols_ref, far_low_ref, far_back_ref, far_member_ref, got_ref, sem
):
    arrive = []
    for i in range(FAR * FOLD // UNFOLD):
        rows = pl.ds(i * UNFOLD, UNFOLD)
        arrive.append(pltpu.make_async_copy(got_hbm.at[rows, :], got_ref.at[rows, :], sem.at[i]))
    for copy in arrive:
        copy.start()
    size = UNFOLD // FOLD
    index = iota((UNFOLD, UNFOLD), 0)
    want = index % size * FOLD + index // size
    pick = jnp.where(iota((UNFOLD, UNFOLD), 1) == want, 1.0, 0.0).astype(bf16)
    for i, copy in enumerate(arrive):
        copy.wait()
        to = slice(i * size, (i + 1) * size)
        block = got_ref[i * UNFOLD : (i + 1) * UNFOLD, :]
        for which, base, part, at, width in CHUNKS:
            rows = dot(pick, block[:, base + at : base + at + width]).astype(bf16)
            out_ref = (far_hidden_ref, far_cols_ref)[which]
            for q in range(FOLD):
                where = slice(q * part + at, q * part + at + width)
                out_ref[to, where] = rows[q * size : (q + 1) * size]
        rows = dot(pick, block[:, WIDTH - RANK : WIDTH]).astype(bf16)
        for q, out_ref in enumerate((far_low_ref, far_back_ref, far_member_ref)):
            out_ref[to, :] = rows[q * size : (q + 1) * size]


def far_kernel(
    far_hidden_ref,
    far_cols_ref,
    far_low_ref,
    far_back_ref,
    far_member_ref,
    cols_ref,
    low_ref,
    back_ref,
    member_ref,
    near_ref,
    sums_ref,
):
    far_hidden, far_cols = far_hidden_ref[...], far_cols_ref[...]
    far_low, far_back, far_member = far_low_ref[...], far_back_ref[...], far_member_ref[...]
    same = 2.0 * cross(far_member, member_ref[...])
    near_ref[...] = same * cross(far_back, back_ref[...])
    near = same * (cross(far_low, low_ref[...]) * cross(far_cols, cols_ref[...]))
    far = cross(far_member, far_member) * (
        cross(far_hidden, far_hidden) * cross(far_back, far_back)
        + cross(far_low, far_low) * cross(far_cols, far_cols)
    )
    sums = jnp.sum(near, axis=1, keepdims=True) + jnp.sum(far, axis=1, keepdims=True)
    sums_ref[...] = jnp.broadcast_to(sums, sums_ref.shape)


def norm_kernel(
    far_hidden_ref, hidden_t_ref, near_ref, sums_ref, far_member_ref, local_ref, norm_ref
):
    near = near_ref[...] * dot(far_hidden_ref[...], hidden_t_ref[...])
    sums = sums_ref[:, :1] + jnp.sum(near, axis=1, keepdims=True)
    far_member = far_member_ref[...].astype(f32)
    norm_ref[...] = local_ref[...] + jnp.sum(far_member * sums, axis=0, keepdims=True)


def finish_kernel(shares_ref, a_ref, b_ref):
    total = jnp.sum(shares_ref[...].astype(f32), axis=0)
    a_ref[0] = total[: UNITS // N_DATA]
    b_ref[0] = total[UNITS // N_DATA :]


def turn_kernel(hidden_ref, cols_ref, hidden_t_ref, cols_t_ref):
    for ref, out_ref in ((hidden_ref, hidden_t_ref), (cols_ref, cols_t_ref)):
        for at in range(0, ref.shape[1], 256):
            out_ref[at : at + 256, :] = ref[:, at : at + 256].T


def user_sums(member, pair):
    same = cross(member, member)
    sums = jnp.sum(same * pair, axis=1)[:, None]
    return jnp.sum(member.astype(f32) * sums, axis=0)[None, :]


def core_split(turned, core_index):
    blocks = turned.reshape(N_Y * N_Z, N_CORE, -1, turned.shape[1])
    return [
        lax.dynamic_index_in_dim(blocks, core, 1, keepdims=False).reshape(-1, turned.shape[1])
        for core in (core_index, 1 - core_index)
    ]


def from_others(part):
    return [
        lax.ppermute(part, "tensor", [(i, (i + k) % N_TENSOR) for i in range(N_TENSOR)])
        for k in (1, 3, 2)
    ]


def flip_tensor(part, flip):
    return lax.ppermute(part, "tensor", [(i, i ^ flip) for i in range(N_TENSOR)])


def per_device(
    hidden,
    upstream,
    adapter_down_weight,
    adapter_up_weight,
    token_user_slot,
    padding_token_mask,
    overflow_user_rows,
    overflow_home_index,
):
    tensor_index = lax.axis_index("tensor")
    core_index = lax.axis_index("core")
    total_users = U_DEV * N_DATA
    clip_norm = CLIP_FACTOR * math.sqrt(RANK * (HIDDEN_UNITS + MODEL_WIDTH))

    def shape(*dims, dtype=bf16):
        return jax.ShapeDtypeStruct(dims, dtype)

    own = tensor_index * COLS
    own_cols = lax.dynamic_slice_in_dim(upstream, own, COLS, 1)
    own_up = lax.dynamic_slice_in_dim(adapter_up_weight, own, COLS, 1)
    rows, home = overflow_user_rows, overflow_home_index
    mask, user = padding_token_mask[None, :], token_user_slot[None, :]
    part, hot = pl.pallas_call(
        lead_kernel,
        out_shape=(shape(SPILL, 2 * RANK, dtype=f32), shape(SPILL, RANK)),
        in_specs=[VMEM] * 7,
        out_specs=(VMEM,) * 2,
        compiler_params=NARROW,
        name="lead",
    )(rows, mask, user, hidden, own_cols, adapter_down_weight, own_up)
    parts = from_others(part)
    send, member = pl.pallas_call(
        dispatch_kernel,
        out_shape=(shape(FAR * FOLD, UNITS_Q + COLS_Q), shape(TOK, RANK)),
        in_specs=[VMEM] * 6,
        out_specs=(VMEM,) * 2,
        scratch_shapes=[pltpu.VMEM(((UNITS_Q + COLS_Q) // RANK, FAR * FOLD, RANK), f32)],
        compiler_params=NARROW,
        name="dispatch",
    )(rows, home, mask, user, hidden, own_cols)
    pair = pl.pallas_call(
        pair_kernel,
        out_shape=shape(FAR * FOLD, RANK),
        in_specs=[VMEM] * 6,
        out_specs=VMEM,
        compiler_params=NARROW,
        name="pair",
    )(part, *parts, hot, home)
    send = jnp.concatenate([send, pair], axis=1)
    send, held_hidden, held_upstream, held_cols = lax.optimization_barrier(
        (send, hidden, upstream, own_cols)
    )
    got = lax.all_to_all(
        send.reshape(N_DATA, SLOT * FOLD, WIDTH), DP, 0, 0, tiled=True
    ).reshape(FAR * FOLD, WIDTH)

    low_part = dot(held_hidden, adapter_down_weight)
    low = sum(from_others(low_part), low_part).astype(bf16)
    back = cross(held_upstream, adapter_up_weight).astype(bf16)
    pair_local = cross(held_hidden, held_hidden) * cross(back, back) + cross(low, low) * cross(
        held_cols, held_cols
    )
    norm_local = user_sums(member, pair_local)
    hidden_turned = held_hidden.T
    hidden_t = core_split(hidden_turned, core_index)
    cols_t = core_split(held_cols.T, core_index)
    got, norm_local, hidden_turned, hidden_t, cols_t = lax.optimization_barrier(
        (got, norm_local, hidden_turned, hidden_t, cols_t)
    )

    far_hidden, far_cols, far_low, far_back, far_member = pl.pallas_call(
        unfold_kernel,
        out_shape=(shape(FAR, UNITS), shape(FAR, COLS)) + (shape(FAR, RANK),) * 3,
        in_specs=[HBM],
        out_specs=(VMEM,) * 5,
        scratch_shapes=[
            pltpu.VMEM((FAR * FOLD, WIDTH), bf16),
            pltpu.SemaphoreType.DMA((FAR * FOLD // UNFOLD,)),
        ],
        compiler_params=NARROW,
        name="unfold",
    )(got)
    near, sums = pl.pallas_call(
        far_kernel,
        out_shape=(shape(FAR, TOK, dtype=f32), shape(FAR, RANK, dtype=f32)),
        in_specs=[VMEM] * 9,
        out_specs=(VMEM,) * 2,
        compiler_params=NARROW,
        name="far",
    )(far_hidden, far_cols, far_low, far_back, far_member, own_cols, low, back, member)
    norm_part = pl.pallas_call(
        norm_kernel,
        out_shape=shape(1, RANK, dtype=f32),
        in_specs=[VMEM] * 6,
        out_specs=VMEM,
        compiler_params=NARROW,
        name="norms",
    )(far_hidden, hidden_turned, near, sums, far_member, norm_local)
    norm_part, far_hidden, far_cols = lax.optimization_barrier((norm_part, far_hidden, far_cols))
    far_hidden_t, far_cols_t = pl.pallas_call(
        turn_kernel,
        out_shape=(shape(UNITS, FAR), shape(COLS, FAR)),
        in_specs=[VMEM] * 2,
        out_specs=(VMEM,) * 2,
        compiler_params=NARROW,
        name="turn",
    )(far_hidden, far_cols)
    far_hidden_t = core_split(far_hidden_t, core_index)
    far_cols_t = core_split(far_cols_t, core_index)
    norm_part = norm_part + flip_tensor(norm_part, 1)
    norm_sq = norm_part + flip_tensor(norm_part, 3)
    factor = clip_norm / jnp.maximum(jnp.sqrt(jnp.maximum(norm_sq, 0.0)), clip_norm)
    weight = jnp.sum(member.astype(f32) * factor, axis=1) / total_users
    far_weight = jnp.sum(far_member.astype(f32) * factor, axis=1) / total_users
    scaled_back = (weight[:, None] * back.astype(f32)).astype(bf16)
    far_scaled_back = (far_weight[:, None] * far_back.astype(f32)).astype(bf16)

    def a_blocks(i, scaled_back):
        total = dot(hidden_t[i], scaled_back) + dot(far_hidden_t[i], far_scaled_back)
        return total.reshape(N_Y * N_Z, -1, RANK)

    def b_blocks(i, low):
        scaled_up = (weight[None, :] * cols_t[i].astype(f32)).astype(bf16)
        far_scaled_up = (far_weight[None, :] * far_cols_t[i].astype(f32)).astype(bf16)
        total = dot(scaled_up, low) + dot(far_scaled_up, far_low)
        return total.reshape(N_Y * N_Z, -1, RANK)

    def from_core(blocks):
        return lax.ppermute(blocks, "core", [(0, 1), (1, 0)])

    other_b = b_blocks(1, low)
    come_b = from_core(other_b)
    held_back, other_b = lax.optimization_barrier((scaled_back, other_b))
    other_a = a_blocks(1, held_back)
    come_a = from_core(other_a)
    held_back, held_low, other_a = lax.optimization_barrier((scaled_back, low, other_a))
    chip_sum = jnp.concatenate(
        [a_blocks(0, held_back) + come_a, b_blocks(0, held_low) + come_b], axis=1
    )
    shares = lax.all_to_all(chip_sum.astype(bf16), ("y", "z"), 0, 0, tiled=True)
    return pl.pallas_call(
        finish_kernel,
        out_shape=(
            shape(1, UNITS // N_DATA, RANK, dtype=f32),
            shape(1, COLS // N_DATA, RANK, dtype=f32),
        ),
        in_specs=[VMEM],
        out_specs=(VMEM,) * 2,
        compiler_params=NARROW,
        name="finish",
    )(shares)


def solution(mesh):
    fine = Mesh(
        mesh.devices.reshape(N_Y, N_Z, N_CORE, N_TENSOR), ("y", "z", "core", "tensor")
    )
    in_specs = (
        P(DP, "tensor"),
        P(DP, None),
        P("tensor", None),
        P(),
        P(DP),
        P(DP),
        P(DP, None),
        P(DP, None),
    )
    out_specs = (P("tensor", DP, None), P("tensor", DP, None))
    return jax.shard_map(
        per_device, mesh=fine, in_specs=in_specs, out_specs=out_specs, check_vma=False
    )
```

```python
import functools
import math

import jax
import jax.numpy as jnp
from jax import lax
from jax.experimental import pallas as pl
from jax.experimental.pallas import tpu as pltpu
from jax.sharding import Mesh, PartitionSpec as P

MODEL_WIDTH = 8192
HIDDEN_UNITS = 14336
RANK = 128
U_DEV = 8
SLOT = 2
CLIP_FACTOR = 4.0
N_Y = 4
N_Z = 8
N_CORE = 2
N_TENSOR = 4
N_DATA = N_Y * N_Z * N_CORE
TOK = 256
FAR = N_DATA * SLOT
FOLD = 4
UNITS = HIDDEN_UNITS // N_TENSOR
COLS = MODEL_WIDTH // N_TENSOR
UNITS_Q = UNITS // FOLD
COLS_Q = COLS // FOLD
DP = ("y", "z", "core")
f32 = jnp.float32
bf16 = jnp.bfloat16
i32 = jnp.int32
VMEM = pl.BlockSpec(memory_space=pltpu.VMEM)
HBM = pl.BlockSpec(memory_space=pltpu.HBM)


def widths(total):
    return [(at, min(256, total - at)) for at in range(0, total, 256)]


NARROW = pltpu.CompilerParams(vmem_limit_bytes=20 * 1024 * 1024)
WIDTH = UNITS_Q + COLS_Q + RANK
SPILL = 64
UNFOLD = 128
CHUNKS = [(0, 0, UNITS_Q, at, width) for at, width in widths(UNITS_Q)] + [
    (1, UNITS_Q, COLS_Q, at, width) for at, width in widths(COLS_Q)
]


def cross(left, right):
    return lax.dot_general(left, right, (((1,), (1,)), ((), ())), preferred_element_type=f32)


def dot(left, right):
    return jnp.dot(left, right, preferred_element_type=f32)


def iota(shape, axis):
    return lax.broadcasted_iota(i32, shape, axis)


def as_column(row):
    size = row.shape[1]
    eye = iota((size, size), 0) == iota((size, size), 1)
    return jnp.sum(jnp.where(eye, row, 0), axis=1, keepdims=True)


def slots_of(home):
    size = home.shape[1]
    earlier = (as_column(home) == home) & (iota((size, size), 0) < iota((size, size), 1))
    return home * SLOT + jnp.sum(earlier.astype(i32), axis=0, keepdims=True)


def lead_kernel(
    rows_ref, mask_ref, user_ref, hidden_ref, cols_ref, down_ref, up_ref, part_ref, hot_ref
):
    listed = as_column(rows_ref[...]) == iota((SPILL, TOK), 1)
    pick = jnp.where(listed & (mask_ref[...] > 0), 1.0, 0.0).astype(bf16)
    user = jnp.where(as_column(user_ref[...]) == iota((TOK, RANK), 1), 1.0, 0.0).astype(bf16)
    hot_ref[...] = dot(pick, user).astype(bf16)
    part_ref[:, :RANK] = dot(dot(pick, hidden_ref[...]).astype(bf16), down_ref[...])
    part_ref[:, RANK:] = cross(dot(pick, cols_ref[...]).astype(bf16), up_ref[...])


def dispatch_kernel(
    rows_ref, home_ref, mask_ref, user_ref, hidden_ref, cols_ref, send_ref, member_ref, wide_ref
):
    slot_of = as_column(slots_of(home_ref[...]))
    hit = as_column(rows_ref[...]) == iota((SPILL, TOK), 1)
    slot = jnp.sum(jnp.where(hit, slot_of + 1, 0), axis=0, keepdims=True) - 1
    real = mask_ref[...] > 0
    pick = jnp.where(iota((FAR, TOK), 0) == jnp.where(real, slot, -1), 1.0, 0.0).astype(bf16)
    for which, base, part, at, width in CHUNKS:
        ref = (hidden_ref, cols_ref)[which]
        for q in range(FOLD):
            rows = dot(pick, ref[:, q * part + at : q * part + at + width])
            for lane in range(0, width, RANK):
                tile = (base + at + lane) // RANK
                wide_ref[tile, pl.ds(q, FAR, stride=FOLD), :] = rows[:, lane : lane + RANK]
        for lane in range(base + at, base + at + width, RANK):
            send_ref[:, lane : lane + RANK] = wide_ref[lane // RANK].astype(bf16)
    user = jnp.where(as_column(user_ref[...]) == iota((TOK, RANK), 1), 1.0, 0.0)
    live = as_column(jnp.where(real & (slot < 0), 1.0, 0.0))
    member_ref[...] = (user * live).astype(bf16)


def pair_kernel(part_ref, first_ref, second_ref, third_ref, hot_ref, home_ref, out_ref):
    total = (part_ref[...] + first_ref[...] + second_ref[...] + third_ref[...]).astype(bf16)
    stacked = jnp.concatenate([total[:, :RANK], total[:, RANK:], hot_ref[...]], axis=0)
    place = iota((FAR * FOLD, SPILL), 0) - slots_of(home_ref[...]) * FOLD
    pick = jnp.concatenate([jnp.where(place == p, 1.0, 0.0) for p in range(3)], axis=1)
    out_ref[...] = dot(pick.astype(bf16), stacked).astype(bf16)


def unfold_kernel(
    got_hbm, far_hidden_ref, far_cols_ref, far_low_ref, far_back_ref, far_member_ref, got_ref, sem
):
    arrive = []
    for i in range(FAR * FOLD // UNFOLD):
        rows = pl.ds(i * UNFOLD, UNFOLD)
        arrive.append(pltpu.make_async_copy(got_hbm.at[rows, :], got_ref.at[rows, :], sem.at[i]))
    for copy in arrive:
        copy.start()
    size = UNFOLD // FOLD
    index = iota((UNFOLD, UNFOLD), 0)
    want = index % size * FOLD + index // size
    pick = jnp.where(iota((UNFOLD, UNFOLD), 1) == want, 1.0, 0.0).astype(bf16)
    for i, copy in enumerate(arrive):
        copy.wait()
        to = slice(i * size, (i + 1) * size)
        block = got_ref[i * UNFOLD : (i + 1) * UNFOLD, :]
        for which, base, part, at, width in CHUNKS:
            rows = dot(pick, block[:, base + at : base + at + width]).astype(bf16)
            out_ref = (far_hidden_ref, far_cols_ref)[which]
            for q in range(FOLD):
                where = slice(q * part + at, q * part + at + width)
                out_ref[to, where] = rows[q * size : (q + 1) * size]
        rows = dot(pick, block[:, WIDTH - RANK : WIDTH]).astype(bf16)
        for q, out_ref in enumerate((far_low_ref, far_back_ref, far_member_ref)):
            out_ref[to, :] = rows[q * size : (q + 1) * size]


def far_kernel(
    far_hidden_ref,
    far_cols_ref,
    far_low_ref,
    far_back_ref,
    far_member_ref,
    cols_ref,
    low_ref,
    back_ref,
    member_ref,
    near_ref,
    sums_ref,
):
    far_hidden, far_cols = far_hidden_ref[...], far_cols_ref[...]
    far_low, far_back, far_member = far_low_ref[...], far_back_ref[...], far_member_ref[...]
    same = 2.0 * cross(far_member, member_ref[...])
    near_ref[...] = same * cross(far_back, back_ref[...])
    near = same * (cross(far_low, low_ref[...]) * cross(far_cols, cols_ref[...]))
    far = cross(far_member, far_member) * (
        cross(far_hidden, far_hidden) * cross(far_back, far_back)
        + cross(far_low, far_low) * cross(far_cols, far_cols)
    )
    sums = jnp.sum(near, axis=1, keepdims=True) + jnp.sum(far, axis=1, keepdims=True)
    sums_ref[...] = jnp.broadcast_to(sums, sums_ref.shape)


def norm_kernel(
    far_hidden_ref, hidden_t_ref, near_ref, sums_ref, far_member_ref, local_ref, norm_ref
):
    near = near_ref[...] * dot(far_hidden_ref[...], hidden_t_ref[...])
    sums = sums_ref[:, :1] + jnp.sum(near, axis=1, keepdims=True)
    far_member = far_member_ref[...].astype(f32)
    norm_ref[...] = local_ref[...] + jnp.sum(far_member * sums, axis=0, keepdims=True)


def finish_kernel(shares_ref, a_ref, b_ref):
    total = jnp.sum(shares_ref[...].astype(f32), axis=0)
    a_ref[0] = total[: UNITS // N_DATA]
    b_ref[0] = total[UNITS // N_DATA :]


def turn_kernel(hidden_ref, cols_ref, hidden_t_ref, cols_t_ref):
    for ref, out_ref in ((hidden_ref, hidden_t_ref), (cols_ref, cols_t_ref)):
        for at in range(0, ref.shape[1], 256):
            out_ref[at : at + 256, :] = ref[:, at : at + 256].T


def user_sums(member, pair):
    same = cross(member, member)
    sums = jnp.sum(same * pair, axis=1)[:, None]
    return jnp.sum(member.astype(f32) * sums, axis=0)[None, :]


def core_split(turned, core_index):
    blocks = turned.reshape(N_Y * N_Z, N_CORE, -1, turned.shape[1])
    return [
        lax.dynamic_index_in_dim(blocks, core, 1, keepdims=False).reshape(-1, turned.shape[1])
        for core in (core_index, 1 - core_index)
    ]


def from_others(part):
    return [
        lax.ppermute(part, "tensor", [(i, (i + k) % N_TENSOR) for i in range(N_TENSOR)])
        for k in (2, 3, 1)
    ]


def flip_tensor(part, flip):
    return lax.ppermute(part, "tensor", [(i, i ^ flip) for i in range(N_TENSOR)])


def per_device(
    hidden,
    upstream,
    adapter_down_weight,
    adapter_up_weight,
    token_user_slot,
    padding_token_mask,
    overflow_user_rows,
    overflow_home_index,
):
    tensor_index = lax.axis_index("tensor")
    core_index = lax.axis_index("core")
    total_users = U_DEV * N_DATA
    clip_norm = CLIP_FACTOR * math.sqrt(RANK * (HIDDEN_UNITS + MODEL_WIDTH))

    def shape(*dims, dtype=bf16):
        return jax.ShapeDtypeStruct(dims, dtype)

    own = tensor_index * COLS
    own_cols = lax.dynamic_slice_in_dim(upstream, own, COLS, 1)
    own_cols, held_up = lax.optimization_barrier((own_cols, adapter_up_weight))
    own_up = lax.dynamic_slice_in_dim(held_up, own, COLS, 1)
    rows, home = overflow_user_rows, overflow_home_index
    mask, user = padding_token_mask[None, :], token_user_slot[None, :]
    part, hot = pl.pallas_call(
        lead_kernel,
        out_shape=(shape(SPILL, 2 * RANK, dtype=f32), shape(SPILL, RANK)),
        in_specs=[VMEM] * 7,
        out_specs=(VMEM,) * 2,
        compiler_params=NARROW,
        name="lead",
    )(rows, mask, user, hidden, own_cols, adapter_down_weight, own_up)
    parts = from_others(part)
    send, member = pl.pallas_call(
        dispatch_kernel,
        out_shape=(shape(FAR * FOLD, UNITS_Q + COLS_Q), shape(TOK, RANK)),
        in_specs=[VMEM] * 6,
        out_specs=(VMEM,) * 2,
        scratch_shapes=[pltpu.VMEM(((UNITS_Q + COLS_Q) // RANK, FAR * FOLD, RANK), f32)],
        compiler_params=NARROW,
        name="dispatch",
    )(rows, home, mask, user, hidden, own_cols)
    pair = pl.pallas_call(
        pair_kernel,
        out_shape=shape(FAR * FOLD, RANK),
        in_specs=[VMEM] * 6,
        out_specs=VMEM,
        compiler_params=NARROW,
        name="pair",
    )(part, *parts, hot, home)
    send = jnp.concatenate([send, pair], axis=1)
    send, held_hidden, held_upstream, held_cols = lax.optimization_barrier(
        (send, hidden, upstream, own_cols)
    )
    got = lax.all_to_all(
        send.reshape(N_DATA, SLOT * FOLD, WIDTH), DP, 0, 0, tiled=True
    ).reshape(FAR * FOLD, WIDTH)

    low_part = dot(held_hidden, adapter_down_weight)
    low = sum(from_others(low_part), low_part).astype(bf16)
    back = cross(held_upstream, adapter_up_weight).astype(bf16)
    pair_local = cross(held_hidden, held_hidden) * cross(back, back) + cross(low, low) * cross(
        held_cols, held_cols
    )
    norm_local = user_sums(member, pair_local)
    hidden_turned = held_hidden.T
    hidden_t = core_split(hidden_turned, core_index)
    cols_t = core_split(held_cols.T, core_index)
    got, norm_local, hidden_turned, hidden_t, cols_t = lax.optimization_barrier(
        (got, norm_local, hidden_turned, hidden_t, cols_t)
    )

    far_hidden, far_cols, far_low, far_back, far_member = pl.pallas_call(
        unfold_kernel,
        out_shape=(shape(FAR, UNITS), shape(FAR, COLS)) + (shape(FAR, RANK),) * 3,
        in_specs=[HBM],
        out_specs=(VMEM,) * 5,
        scratch_shapes=[
            pltpu.VMEM((FAR * FOLD, WIDTH), bf16),
            pltpu.SemaphoreType.DMA((FAR * FOLD // UNFOLD,)),
        ],
        compiler_params=NARROW,
        name="unfold",
    )(got)
    near, sums = pl.pallas_call(
        far_kernel,
        out_shape=(shape(FAR, TOK, dtype=f32), shape(FAR, RANK, dtype=f32)),
        in_specs=[VMEM] * 9,
        out_specs=(VMEM,) * 2,
        compiler_params=NARROW,
        name="far",
    )(far_hidden, far_cols, far_low, far_back, far_member, own_cols, low, back, member)
    norm_part = pl.pallas_call(
        norm_kernel,
        out_shape=shape(1, RANK, dtype=f32),
        in_specs=[VMEM] * 6,
        out_specs=VMEM,
        compiler_params=NARROW,
        name="norms",
    )(far_hidden, hidden_turned, near, sums, far_member, norm_local)
    norm_part, far_hidden, far_cols = lax.optimization_barrier((norm_part, far_hidden, far_cols))
    far_hidden_t, far_cols_t = pl.pallas_call(
        turn_kernel,
        out_shape=(shape(UNITS, FAR), shape(COLS, FAR)),
        in_specs=[VMEM] * 2,
        out_specs=(VMEM,) * 2,
        compiler_params=NARROW,
        name="turn",
    )(far_hidden, far_cols)
    far_hidden_t = core_split(far_hidden_t, core_index)
    far_cols_t = core_split(far_cols_t, core_index)
    norm_part = norm_part + flip_tensor(norm_part, 1)
    norm_sq = norm_part + flip_tensor(norm_part, 3)
    factor = clip_norm / jnp.maximum(jnp.sqrt(jnp.maximum(norm_sq, 0.0)), clip_norm)
    weight = jnp.sum(member.astype(f32) * factor, axis=1) / total_users
    far_weight = jnp.sum(far_member.astype(f32) * factor, axis=1) / total_users
    scaled_back = (weight[:, None] * back.astype(f32)).astype(bf16)
    far_scaled_back = (far_weight[:, None] * far_back.astype(f32)).astype(bf16)

    def a_blocks(i, scaled_back):
        total = dot(hidden_t[i], scaled_back) + dot(far_hidden_t[i], far_scaled_back)
        return total.reshape(N_Y * N_Z, -1, RANK)

    def b_blocks(i, low):
        scaled_up = (weight[None, :] * cols_t[i].astype(f32)).astype(bf16)
        far_scaled_up = (far_weight[None, :] * far_cols_t[i].astype(f32)).astype(bf16)
        total = dot(scaled_up, low) + dot(far_scaled_up, far_low)
        return total.reshape(N_Y * N_Z, -1, RANK)

    def from_core(blocks):
        return lax.ppermute(blocks, "core", [(0, 1), (1, 0)])

    other_b = b_blocks(1, low)
    come_b = from_core(other_b)
    held_back, other_b = lax.optimization_barrier((scaled_back, other_b))
    other_a = a_blocks(1, held_back)
    come_a = from_core(other_a)
    held_back, held_low, other_a = lax.optimization_barrier((scaled_back, low, other_a))
    chip_sum = jnp.concatenate(
        [a_blocks(0, held_back) + come_a, b_blocks(0, held_low) + come_b], axis=1
    )
    shares = lax.all_to_all(chip_sum.astype(bf16), ("y", "z"), 0, 0, tiled=True)
    return pl.pallas_call(
        finish_kernel,
        out_shape=(
            shape(1, UNITS // N_DATA, RANK, dtype=f32),
            shape(1, COLS // N_DATA, RANK, dtype=f32),
        ),
        in_specs=[VMEM],
        out_specs=(VMEM,) * 2,
        compiler_params=NARROW,
        name="finish",
    )(shares)


def solution(mesh):
    fine = Mesh(
        mesh.devices.reshape(N_Y, N_Z, N_CORE, N_TENSOR), ("y", "z", "core", "tensor")
    )
    in_specs = (
        P(DP, "tensor"),
        P(DP, None),
        P("tensor", None),
        P(),
        P(DP),
        P(DP),
        P(DP, None),
        P(DP, None),
    )
    out_specs = (P("tensor", DP, None), P("tensor", DP, None))
    return jax.shard_map(
        per_device, mesh=fine, in_specs=in_specs, out_specs=out_specs, check_vma=False
    )
```

```python
import functools
import math

import jax
import jax.numpy as jnp
from jax import lax
from jax.experimental import pallas as pl
from jax.experimental.pallas import tpu as pltpu
from jax.sharding import Mesh, PartitionSpec as P

MODEL_WIDTH = 8192
HIDDEN_UNITS = 14336
RANK = 128
U_DEV = 8
SLOT = 2
CLIP_FACTOR = 4.0
N_Y = 4
N_Z = 8
N_CORE = 2
N_TENSOR = 4
N_DATA = N_Y * N_Z * N_CORE
TOK = 256
FAR = N_DATA * SLOT
FOLD = 4
UNITS = HIDDEN_UNITS // N_TENSOR
COLS = MODEL_WIDTH // N_TENSOR
UNITS_Q = UNITS // FOLD
COLS_Q = COLS // FOLD
DP = ("y", "z", "core")
f32 = jnp.float32
bf16 = jnp.bfloat16
i32 = jnp.int32
VMEM = pl.BlockSpec(memory_space=pltpu.VMEM)
HBM = pl.BlockSpec(memory_space=pltpu.HBM)


def widths(total):
    return [(at, min(256, total - at)) for at in range(0, total, 256)]


NARROW = pltpu.CompilerParams(vmem_limit_bytes=20 * 1024 * 1024)
WIDTH = UNITS_Q + COLS_Q + RANK
SPILL = 64
UNFOLD = 128
CHUNKS = [(0, 0, UNITS_Q, at, width) for at, width in widths(UNITS_Q)] + [
    (1, UNITS_Q, COLS_Q, at, width) for at, width in widths(COLS_Q)
]


def cross(left, right):
    return lax.dot_general(left, right, (((1,), (1,)), ((), ())), preferred_element_type=f32)


def dot(left, right):
    return jnp.dot(left, right, preferred_element_type=f32)


def iota(shape, axis):
    return lax.broadcasted_iota(i32, shape, axis)


def as_column(row):
    size = row.shape[1]
    eye = iota((size, size), 0) == iota((size, size), 1)
    return jnp.sum(jnp.where(eye, row, 0), axis=1, keepdims=True)


def slots_of(home):
    size = home.shape[1]
    earlier = (as_column(home) == home) & (iota((size, size), 0) < iota((size, size), 1))
    return home * SLOT + jnp.sum(earlier.astype(i32), axis=0, keepdims=True)


def lead_kernel(
    rows_ref, mask_ref, user_ref, hidden_ref, cols_ref, down_ref, up_ref, part_ref, hot_ref
):
    listed = as_column(rows_ref[...]) == iota((SPILL, TOK), 1)
    pick = jnp.where(listed & (mask_ref[...] > 0), 1.0, 0.0).astype(bf16)
    user = jnp.where(as_column(user_ref[...]) == iota((TOK, RANK), 1), 1.0, 0.0).astype(bf16)
    hot_ref[...] = dot(pick, user).astype(bf16)
    part_ref[:, :RANK] = dot(dot(pick, hidden_ref[...]).astype(bf16), down_ref[...])
    part_ref[:, RANK:] = cross(dot(pick, cols_ref[...]).astype(bf16), up_ref[...])


def dispatch_kernel(
    rows_ref, home_ref, mask_ref, user_ref, hidden_ref, cols_ref, send_ref, member_ref, wide_ref
):
    slot_of = as_column(slots_of(home_ref[...]))
    hit = as_column(rows_ref[...]) == iota((SPILL, TOK), 1)
    slot = jnp.sum(jnp.where(hit, slot_of + 1, 0), axis=0, keepdims=True) - 1
    real = mask_ref[...] > 0
    pick = jnp.where(iota((FAR, TOK), 0) == jnp.where(real, slot, -1), 1.0, 0.0).astype(bf16)
    for which, base, part, at, width in CHUNKS:
        ref = (hidden_ref, cols_ref)[which]
        for q in range(FOLD):
            rows = dot(pick, ref[:, q * part + at : q * part + at + width])
            for lane in range(0, width, RANK):
                tile = (base + at + lane) // RANK
                wide_ref[tile, pl.ds(q, FAR, stride=FOLD), :] = rows[:, lane : lane + RANK]
        for lane in range(base + at, base + at + width, RANK):
            send_ref[:, lane : lane + RANK] = wide_ref[lane // RANK].astype(bf16)
    user = jnp.where(as_column(user_ref[...]) == iota((TOK, RANK), 1), 1.0, 0.0)
    live = as_column(jnp.where(real & (slot < 0), 1.0, 0.0))
    member_ref[...] = (user * live).astype(bf16)


def pair_kernel(part_ref, first_ref, second_ref, third_ref, hot_ref, home_ref, out_ref):
    total = (part_ref[...] + first_ref[...] + second_ref[...] + third_ref[...]).astype(bf16)
    stacked = jnp.concatenate([total[:, :RANK], total[:, RANK:], hot_ref[...]], axis=0)
    place = iota((FAR * FOLD, SPILL), 0) - slots_of(home_ref[...]) * FOLD
    pick = jnp.concatenate([jnp.where(place == p, 1.0, 0.0) for p in range(3)], axis=1)
    out_ref[...] = dot(pick.astype(bf16), stacked).astype(bf16)


def unfold_kernel(
    got_hbm, far_hidden_ref, far_cols_ref, far_low_ref, far_back_ref, far_member_ref, got_ref, sem
):
    arrive = []
    for i in range(FAR * FOLD // UNFOLD):
        rows = pl.ds(i * UNFOLD, UNFOLD)
        arrive.append(pltpu.make_async_copy(got_hbm.at[rows, :], got_ref.at[rows, :], sem.at[i]))
    for copy in arrive:
        copy.start()
    size = UNFOLD // FOLD
    index = iota((UNFOLD, UNFOLD), 0)
    want = index % size * FOLD + index // size
    pick = jnp.where(iota((UNFOLD, UNFOLD), 1) == want, 1.0, 0.0).astype(bf16)
    for i, copy in enumerate(arrive):
        copy.wait()
        to = slice(i * size, (i + 1) * size)
        block = got_ref[i * UNFOLD : (i + 1) * UNFOLD, :]
        for which, base, part, at, width in CHUNKS:
            rows = dot(pick, block[:, base + at : base + at + width]).astype(bf16)
            out_ref = (far_hidden_ref, far_cols_ref)[which]
            for q in range(FOLD):
                where = slice(q * part + at, q * part + at + width)
                out_ref[to, where] = rows[q * size : (q + 1) * size]
        rows = dot(pick, block[:, WIDTH - RANK : WIDTH]).astype(bf16)
        for q, out_ref in enumerate((far_low_ref, far_back_ref, far_member_ref)):
            out_ref[to, :] = rows[q * size : (q + 1) * size]


def far_kernel(
    far_hidden_ref,
    far_cols_ref,
    far_low_ref,
    far_back_ref,
    far_member_ref,
    cols_ref,
    low_ref,
    back_ref,
    member_ref,
    near_ref,
    sums_ref,
):
    far_hidden, far_cols = far_hidden_ref[...], far_cols_ref[...]
    far_low, far_back, far_member = far_low_ref[...], far_back_ref[...], far_member_ref[...]
    same = 2.0 * cross(far_member, member_ref[...])
    near_ref[...] = same * cross(far_back, back_ref[...])
    near = same * (cross(far_low, low_ref[...]) * cross(far_cols, cols_ref[...]))
    far = cross(far_member, far_member) * (
        cross(far_hidden, far_hidden) * cross(far_back, far_back)
        + cross(far_low, far_low) * cross(far_cols, far_cols)
    )
    sums = jnp.sum(near, axis=1, keepdims=True) + jnp.sum(far, axis=1, keepdims=True)
    sums_ref[...] = jnp.broadcast_to(sums, sums_ref.shape)


def norm_kernel(
    far_hidden_ref, hidden_t_ref, near_ref, sums_ref, far_member_ref, local_ref, norm_ref
):
    near = near_ref[...] * dot(far_hidden_ref[...], hidden_t_ref[...])
    sums = sums_ref[:, :1] + jnp.sum(near, axis=1, keepdims=True)
    far_member = far_member_ref[...].astype(f32)
    norm_ref[...] = local_ref[...] + jnp.sum(far_member * sums, axis=0, keepdims=True)


def finish_kernel(shares_ref, a_ref, b_ref):
    total = jnp.sum(shares_ref[...].astype(f32), axis=0)
    a_ref[0] = total[: UNITS // N_DATA]
    b_ref[0] = total[UNITS // N_DATA :]


def turn_kernel(hidden_ref, cols_ref, hidden_t_ref, cols_t_ref):
    for ref, out_ref in ((hidden_ref, hidden_t_ref), (cols_ref, cols_t_ref)):
        for at in range(0, ref.shape[1], 256):
            out_ref[at : at + 256, :] = ref[:, at : at + 256].T


def user_sums(member, pair):
    same = cross(member, member)
    sums = jnp.sum(same * pair, axis=1)[:, None]
    return jnp.sum(member.astype(f32) * sums, axis=0)[None, :]


def core_split(turned, core_index):
    blocks = turned.reshape(N_Y * N_Z, N_CORE, -1, turned.shape[1])
    return [
        lax.dynamic_index_in_dim(blocks, core, 1, keepdims=False).reshape(-1, turned.shape[1])
        for core in (core_index, 1 - core_index)
    ]


def from_others(part):
    return [
        lax.ppermute(part, "tensor", [(i, (i + k) % N_TENSOR) for i in range(N_TENSOR)])
        for k in (2, 3, 1)
    ]


def flip_tensor(part, flip):
    return lax.ppermute(part, "tensor", [(i, i ^ flip) for i in range(N_TENSOR)])


def per_device(
    hidden,
    upstream,
    adapter_down_weight,
    adapter_up_weight,
    token_user_slot,
    padding_token_mask,
    overflow_user_rows,
    overflow_home_index,
):
    tensor_index = lax.axis_index("tensor")
    core_index = lax.axis_index("core")
    total_users = U_DEV * N_DATA
    clip_norm = CLIP_FACTOR * math.sqrt(RANK * (HIDDEN_UNITS + MODEL_WIDTH))

    def shape(*dims, dtype=bf16):
        return jax.ShapeDtypeStruct(dims, dtype)

    own = tensor_index * COLS
    own_cols = lax.dynamic_slice_in_dim(upstream, own, COLS, 1)
    own_cols, held_up = lax.optimization_barrier((own_cols, adapter_up_weight))
    own_up = lax.dynamic_slice_in_dim(held_up, own, COLS, 1)
    rows, home = overflow_user_rows, overflow_home_index
    mask, user = padding_token_mask[None, :], token_user_slot[None, :]
    part, hot = pl.pallas_call(
        lead_kernel,
        out_shape=(shape(SPILL, 2 * RANK, dtype=f32), shape(SPILL, RANK)),
        in_specs=[VMEM] * 7,
        out_specs=(VMEM,) * 2,
        compiler_params=NARROW,
        name="lead",
    )(rows, mask, user, hidden, own_cols, adapter_down_weight, own_up)
    parts = from_others(part)
    send, member = pl.pallas_call(
        dispatch_kernel,
        out_shape=(shape(FAR * FOLD, UNITS_Q + COLS_Q), shape(TOK, RANK)),
        in_specs=[VMEM] * 6,
        out_specs=(VMEM,) * 2,
        scratch_shapes=[pltpu.VMEM(((UNITS_Q + COLS_Q) // RANK, FAR * FOLD, RANK), f32)],
        compiler_params=NARROW,
        name="dispatch",
    )(rows, home, mask, user, hidden, own_cols)
    pair = pl.pallas_call(
        pair_kernel,
        out_shape=shape(FAR * FOLD, RANK),
        in_specs=[VMEM] * 6,
        out_specs=VMEM,
        compiler_params=NARROW,
        name="pair",
    )(part, *parts, hot, home)
    send = jnp.concatenate([send, pair], axis=1)
    send, held_hidden, held_upstream, held_cols = lax.optimization_barrier(
        (send, hidden, upstream, own_cols)
    )
    got = lax.all_to_all(
        send.reshape(N_DATA, SLOT * FOLD, WIDTH), DP, 0, 0, tiled=True
    ).reshape(FAR * FOLD, WIDTH)

    low_part = dot(held_hidden, adapter_down_weight)
    low = sum(from_others(low_part), low_part).astype(bf16)
    back = cross(held_upstream, adapter_up_weight).astype(bf16)
    pair_local = cross(held_hidden, held_hidden) * cross(back, back) + cross(low, low) * cross(
        held_cols, held_cols
    )
    norm_local = user_sums(member, pair_local)
    hidden_turned = held_hidden.T
    hidden_t = core_split(hidden_turned, core_index)
    cols_t = core_split(held_cols.T, core_index)
    got, norm_local, hidden_turned, hidden_t, cols_t = lax.optimization_barrier(
        (got, norm_local, hidden_turned, hidden_t, cols_t)
    )

    far_hidden, far_cols, far_low, far_back, far_member = pl.pallas_call(
        unfold_kernel,
        out_shape=(shape(FAR, UNITS), shape(FAR, COLS)) + (shape(FAR, RANK),) * 3,
        in_specs=[HBM],
        out_specs=(VMEM,) * 5,
        scratch_shapes=[
            pltpu.VMEM((FAR * FOLD, WIDTH), bf16),
            pltpu.SemaphoreType.DMA((FAR * FOLD // UNFOLD,)),
        ],
        compiler_params=NARROW,
        name="unfold",
    )(got)
    near, sums = pl.pallas_call(
        far_kernel,
        out_shape=(shape(FAR, TOK, dtype=f32), shape(FAR, RANK, dtype=f32)),
        in_specs=[VMEM] * 9,
        out_specs=(VMEM,) * 2,
        compiler_params=NARROW,
        name="far",
    )(far_hidden, far_cols, far_low, far_back, far_member, own_cols, low, back, member)
    norm_part = pl.pallas_call(
        norm_kernel,
        out_shape=shape(1, RANK, dtype=f32),
        in_specs=[VMEM] * 6,
        out_specs=VMEM,
        compiler_params=NARROW,
        name="norms",
    )(far_hidden, hidden_turned, near, sums, far_member, norm_local)
    norm_part, far_hidden, far_cols = lax.optimization_barrier((norm_part, far_hidden, far_cols))
    far_hidden_t, far_cols_t = pl.pallas_call(
        turn_kernel,
        out_shape=(shape(UNITS, FAR), shape(COLS, FAR)),
        in_specs=[VMEM] * 2,
        out_specs=(VMEM,) * 2,
        compiler_params=NARROW,
        name="turn",
    )(far_hidden, far_cols)
    far_hidden_t = core_split(far_hidden_t, core_index)
    far_cols_t = core_split(far_cols_t, core_index)
    norm_part = norm_part + flip_tensor(norm_part, 1)
    norm_sq = norm_part + flip_tensor(norm_part, 2)
    factor = clip_norm / jnp.maximum(jnp.sqrt(jnp.maximum(norm_sq, 0.0)), clip_norm)
    weight = jnp.sum(member.astype(f32) * factor, axis=1) / total_users
    far_weight = jnp.sum(far_member.astype(f32) * factor, axis=1) / total_users
    scaled_back = (weight[:, None] * back.astype(f32)).astype(bf16)
    far_scaled_back = (far_weight[:, None] * far_back.astype(f32)).astype(bf16)

    def a_blocks(i, scaled_back):
        total = dot(hidden_t[i], scaled_back) + dot(far_hidden_t[i], far_scaled_back)
        return total.reshape(N_Y * N_Z, -1, RANK)

    def b_blocks(i, low):
        scaled_up = (weight[None, :] * cols_t[i].astype(f32)).astype(bf16)
        far_scaled_up = (far_weight[None, :] * far_cols_t[i].astype(f32)).astype(bf16)
        total = dot(scaled_up, low) + dot(far_scaled_up, far_low)
        return total.reshape(N_Y * N_Z, -1, RANK)

    def from_core(blocks):
        return lax.ppermute(blocks, "core", [(0, 1), (1, 0)])

    other_b = b_blocks(1, low)
    come_b = from_core(other_b)
    held_back, other_b = lax.optimization_barrier((scaled_back, other_b))
    other_a = a_blocks(1, held_back)
    come_a = from_core(other_a)
    held_back, held_low, other_a = lax.optimization_barrier((scaled_back, low, other_a))
    chip_sum = jnp.concatenate(
        [a_blocks(0, held_back) + come_a, b_blocks(0, held_low) + come_b], axis=1
    )
    shares = lax.all_to_all(chip_sum.astype(bf16), ("y", "z"), 0, 0, tiled=True)
    return pl.pallas_call(
        finish_kernel,
        out_shape=(
            shape(1, UNITS // N_DATA, RANK, dtype=f32),
            shape(1, COLS // N_DATA, RANK, dtype=f32),
        ),
        in_specs=[VMEM],
        out_specs=(VMEM,) * 2,
        compiler_params=NARROW,
        name="finish",
    )(shares)


def solution(mesh):
    fine = Mesh(
        mesh.devices.reshape(N_Y, N_Z, N_CORE, N_TENSOR), ("y", "z", "core", "tensor")
    )
    in_specs = (
        P(DP, "tensor"),
        P(DP, None),
        P("tensor", None),
        P(),
        P(DP),
        P(DP),
        P(DP, None),
        P(DP, None),
    )
    out_specs = (P("tensor", DP, None), P("tensor", DP, None))
    return jax.shard_map(
        per_device, mesh=fine, in_specs=in_specs, out_specs=out_specs, check_vma=False
    )
```
